32 devices in a mesh: grp: 2 (over y), row: 4 (over x, core), col: 4 (over z).
Axes of the slice: x: 2, y: 2, z: 4, core: 2. Of those that a mesh axis runs over, the one named last changes fastest.
Arguments:
- alignment: bfloat16 [192, 256, 256], P('grp', 'row'), parts along dimension 0, may hold values from -6 to 6
- coverage: int32 [192, 256], P('grp', 'row'), parts along dimension 0, may hold values from 0 to 1, as said below
- layer_norm_gain: float32 [256], replicated, may hold values from 0.25 to 1.75
- layer_norm_bias: float32 [256], replicated, may hold values from -3 to 3
- left_weight: bfloat16 [256, 32], replicated, may hold values from -0.375 to 0.375
- right_weight: bfloat16 [256, 32], replicated, may hold values from -0.375 to 0.375
- out_weight: bfloat16 [1024, 128], replicated, may hold values from -1.5 to 1.5
- out_bias: float32 [128], replicated, may hold values from -3 to 3
- cotangent: bfloat16 [512, 256, 128], P(('grp', 'row'), 'col'), parts along dimension 0, may hold values from -6 to 6
Outputs:
- pair_update: bfloat16 [512, 256, 128], P(('grp', 'row'), 'col'), parts along dimension 0
- sequence_alignment_gradient: bfloat16 [192, 256, 256], P('grp', 'row'), parts along dimension 0
- grad_left: float32 [512, 32], P('grp'), parts along dimension 0
- grad_right: float32 [512, 32], P('grp'), parts along dimension 0
- grad_out: float32 [2048, 128], P('grp'), parts along dimension 0
The draws below stay inside these ranges and needn't reach their ends.
There are 2 independent parts, one for each index of `grp`. The reference program is written for one: setup_inputs(seed, part) draws one part's arguments, and reference() takes and returns one part's arrays. A program takes and returns all parts, laid end to end along the dimension named above; an argument that names none is the same for every part. Nothing has to cross between parts.
Inputs may be any that keep to these rules, and one draw needn't show every extreme that they name: `coverage`: for each residue the mask is 1 on a leading run of MSA rows (possibly empty) and 0 after it.
All inputs are finite; a program needn't handle non-finite values.
Results may differ from the reference program's by a relative error of at most 0.0073.
Values may be sent and summed in bfloat16 or wider, within the bound.
No kernel may reach another device: no remote copies, remote signals or barrier semaphores. Data moves between devices by JAX's collectives and lax.ppermute only.
A program may use at most 128 MiB of HBM per device.

```python
import jax
import jax.numpy as jnp
from jax import lax

C = 256
PROJ = 32
PAIR = 128
SEQS = 96
RES_ROW = 64
RES = 256


def draw_coverage(key, part):
    key = jax.random.fold_in(key, 7)
    depth = jax.random.randint(key, (RES,), -(SEQS // 8), SEQS + 1)
    depth = jnp.maximum(depth, 0)
    positions = jnp.arange(SEQS)[:, None]
    return (positions < depth[None, :]).astype(jnp.int32)


def block_scale(key, shape, cuts, smallest, top_value):
    def one(dim, parts):
        steps = jax.random.uniform(jax.random.fold_in(jax.random.fold_in(key, 6), dim), (parts,), jnp.float32, smallest / len(cuts), top_value / len(cuts))
        return jnp.repeat(jnp.exp(steps), shape[dim] // parts).reshape((-1,) + (1,) * (len(shape) - dim - 1))

    gain = one(*cuts[0])
    for cut in cuts[1:]:
        gain = gain * one(*cut)
    return gain


def bell_draw(rng, dims, scale, bound, split=(), held_as=jnp.bfloat16):
    result = jax.random.normal(rng, dims, jnp.float32) * scale
    if len(split) > 0:
        result = block_scale(rng, dims, split, -0.22, 0.18) * result
    return jnp.clip(result, min=-bound, max=bound).astype(held_as)


def setup_inputs(seed: int = 0, part: int = 0) -> dict:
    seeds = jax.random.split(jax.random.key(seed), 10)
    own_keys = jax.random.split(jax.random.fold_in(seeds[9], part), 10)
    return {
        "alignment": bell_draw(own_keys[0], (SEQS, RES, C), 1.0, 6.0, ((1, 4),)),
        "coverage": draw_coverage(jax.random.fold_in(jax.random.fold_in(seeds[9], part), 71), part),
        "layer_norm_gain": jnp.clip(1.0 + 0.15 * jax.random.normal(seeds[2], (C,), jnp.float32), 0.25, 1.75),
        "layer_norm_bias": bell_draw(seeds[3], (C,), 0.5, 3.0, (), jnp.float32),
        "left_weight": bell_draw(seeds[4], (C, PROJ), C ** -0.5, 0.375),
        "right_weight": bell_draw(seeds[5], (C, PROJ), C ** -0.5, 0.375),
        "out_weight": bell_draw(seeds[6], (PROJ * PROJ, PAIR), 16 ** -0.5, 1.5),
        "out_bias": bell_draw(seeds[7], (PAIR,), 0.5, 3.0, (), jnp.float32),
        "cotangent": bell_draw(own_keys[8], (RES, RES, PAIR), 1.0, 6.0, ((0, 4), (1, 4))),
    }


def reference(alignment, coverage, layer_norm_gain, layer_norm_bias, left_weight, right_weight, out_weight, out_bias, cotangent):
    maskf = coverage.astype(jnp.float32)
    values = alignment.astype(jnp.float32)
    centered_values = values - lax.optimization_barrier(jnp.mean(values, axis=-1, keepdims=True))
    inverse_deviation = lax.rsqrt(lax.optimization_barrier(jnp.mean(centered_values * centered_values, axis=-1, keepdims=True)) + 1e-05)
    standardized_input = centered_values * inverse_deviation
    normalized_input = (standardized_input * layer_norm_gain + layer_norm_bias).astype(jnp.bfloat16)
    normed_f = normalized_input.astype(jnp.float32)
    left = (jnp.einsum('src,cd->srd', normed_f, left_weight.astype(jnp.float32)) * maskf[..., None]).astype(jnp.bfloat16)
    right = (jnp.einsum('src,cd->srd', normed_f, right_weight.astype(jnp.float32)) * maskf[..., None]).astype(jnp.bfloat16)
    left_f = left.astype(jnp.float32)
    right_f = right.astype(jnp.float32)
    counts = jnp.einsum('si,sj->ij', maskf, maskf)
    denom = jnp.maximum(counts, 1.0)
    wout_f = out_weight.astype(jnp.float32)
    blocks = RES // RES_ROW
    wide = PROJ * PROJ

    def step(carry, index):
        grad_w, grad_r = carry
        start = (index * RES_ROW).astype(jnp.int32)
        left_blk = lax.dynamic_slice_in_dim(left_f, start, RES_ROW, 1)
        den_blk = lax.dynamic_slice_in_dim(denom, start, RES_ROW, 0)
        cot_blk = lax.dynamic_slice_in_dim(cotangent, start, RES_ROW, 0).astype(jnp.float32)
        outer = jnp.einsum('sic,sjd->ijcd', left_blk, right_f).astype(jnp.bfloat16).reshape(RES_ROW, RES, wide)
        outer_f = outer.astype(jnp.float32)
        proj = jnp.einsum('ijf,fh->ijh', outer_f, wout_f)
        update = ((proj + out_bias) / den_blk[..., None]).astype(jnp.bfloat16)
        scaled = (cot_blk / den_blk[..., None]).astype(jnp.bfloat16).astype(jnp.float32)
        grad_w = grad_w + jnp.einsum('ijf,ijh->fh', outer_f, scaled)
        grad_outer = jnp.einsum('ijh,fh->ijf', scaled, wout_f).astype(jnp.bfloat16).astype(jnp.float32)
        grad_outer = grad_outer.reshape(RES_ROW, RES, PROJ, PROJ)
        grad_l = jnp.einsum('ijcd,sjd->sic', grad_outer, right_f)
        grad_r = grad_r + jnp.einsum('ijcd,sic->sjd', grad_outer, left_blk)
        return ((grad_w, grad_r), (update, grad_l))
    init = (jnp.zeros((wide, PAIR), jnp.float32), jnp.zeros((SEQS, RES, PROJ), jnp.float32))
    (grad_out, right_sum), (updates, left_parts) = lax.scan(step, init, jnp.arange(blocks, dtype=jnp.int32))
    pair_update = updates.reshape(RES, RES, PAIR)
    left_sum = jnp.transpose(left_parts, (1, 0, 2, 3)).reshape(SEQS, RES, PROJ)
    grad_left_side = (left_sum * maskf[..., None]).astype(jnp.bfloat16).astype(jnp.float32)
    grad_right_side = (right_sum * maskf[..., None]).astype(jnp.bfloat16).astype(jnp.float32)
    grad_left = jnp.einsum('src,srd->cd', normed_f, grad_left_side)
    grad_right = jnp.einsum('src,srd->cd', normed_f, grad_right_side)
    grad_normed = jnp.einsum('srd,cd->src', grad_left_side, left_weight.astype(jnp.float32)) + jnp.einsum('srd,cd->src', grad_right_side, right_weight.astype(jnp.float32))
    gain_scaled_gradient = grad_normed * layer_norm_gain
    sequence_alignment_gradient = inverse_deviation * (gain_scaled_gradient - lax.optimization_barrier(jnp.mean(gain_scaled_gradient, axis=-1, keepdims=True)) - standardized_input * lax.optimization_barrier(jnp.mean(gain_scaled_gradient * standardized_input, axis=-1, keepdims=True)))
    return (pair_update, sequence_alignment_gradient.astype(jnp.bfloat16), grad_left, grad_right, grad_out)
```

```python
import functools

import jax
import jax.numpy as jnp
from jax import lax
from jax.experimental import pallas as pl
from jax.experimental.pallas import tpu as pltpu
from jax.sharding import PartitionSpec as P

BF = jnp.bfloat16
F32 = jnp.float32
VMEM_LIMIT = 50 * 1024 * 1024
NT = (((1,), (1,)), ((), ()))
TN = (((0,), (0,)), ((), ()))


def params():
    return pltpu.CompilerParams(vmem_limit_bytes=VMEM_LIMIT)


def dot(a, b, dims=(((1,), (0,)), ((), ()))):
    return lax.dot_general(a, b, dims, preferred_element_type=F32)


def whole(shape):
    return pl.BlockSpec(shape, lambda *_: (0,) * len(shape))


def project_kernel(
    depth_ref, x_ref, depth_row, gain, bias, wl, wrt, normed_ref, r_ref, l_ref, lt_ref, ys, zl
):
    n = pl.program_id(0)
    steps = pl.num_programs(0)
    _, g_blk, rows, chans = x_ref.shape
    narrow = wrt.shape[0]
    half = g_blk * steps
    gain_v = gain[...]
    bias_v = bias[...]
    for g in range(g_blk):
        both = []
        for s2 in range(2):
            x = x_ref[s2, g].astype(F32)
            c = x - jnp.mean(x, axis=-1, keepdims=True)
            inv = lax.rsqrt(jnp.mean(c * c, axis=-1, keepdims=True) + 1e-05)
            nb = (c * inv * gain_v + bias_v).astype(BF)
            normed_ref[s2, g] = nb
            both.append(nb)
        pair = jnp.concatenate(both, axis=0)
        at = n * g_blk + g
        ys[pl.ds(pl.multiple_of(at * narrow, narrow), narrow), :] = dot(wrt[...], pair, NT)
        z = dot(pair, wl[...])
        zl[pl.ds(pl.multiple_of(at * rows, rows), rows), :] = z[:rows]
        zl[pl.ds(pl.multiple_of((half + at) * rows, rows), rows), :] = z[rows:]

    @pl.when(n == steps - 1)
    def _():
        lane = lax.broadcasted_iota(jnp.int32, (half, 2 * rows), 1)
        row = lax.broadcasted_iota(jnp.int32, (half, 2 * rows), 0).astype(F32)
        low = lane < rows
        dep = depth_row[...]
        top_on = row < dep
        bot_on = row + half < dep
        for dp in range(narrow // 2):
            even = ys[pl.ds(2 * dp, half, stride=narrow), :]
            odd = ys[pl.ds(2 * dp + 1, half, stride=narrow), :]
            top = jnp.where(low, even, pltpu.roll(odd, rows, 1))
            bot = jnp.where(low, pltpu.roll(even, rows, 1), odd)
            at = slice(dp * 2 * rows, (dp + 1) * 2 * rows)
            r_ref[0:half, at] = jnp.where(top_on, top, 0.0).astype(BF)
            r_ref[half : 2 * half, at] = jnp.where(bot_on, bot, 0.0).astype(BF)
        seq = lax.broadcasted_iota(jnp.int32, (2 * half, narrow), 0)
        per = 128 // narrow
        for q in range(rows // per):
            parts = []
            for k in range(per):
                i = q * per + k
                v = zl[pl.ds(i, 2 * half, stride=rows), :]
                parts.append(jnp.where(seq < depth_ref[i], v, 0.0))
            tile = jnp.concatenate(parts, axis=1)
            l_ref[:, q * 128 : (q + 1) * 128] = tile.astype(BF)
            lt_ref[q * 128 : (q + 1) * 128, :] = tile.T.astype(BF)


def project(depth, alignment, gain, bias, wl, wr):
    seqs, rows, chans = alignment.shape
    narrow = wl.shape[1]
    half = seqs // 2
    g_blk = 8
    steps = half // g_blk
    wide = rows * narrow
    depth_row = jnp.tile(depth.astype(F32), 2)[None, :]
    blk = pl.BlockSpec((2, g_blk, rows, chans), lambda n, *_: (0, n, 0, 0))
    outs = (
        jax.ShapeDtypeStruct((2, half, rows, chans), BF),
        jax.ShapeDtypeStruct((seqs, wide), BF),
        jax.ShapeDtypeStruct((seqs, wide), BF),
        jax.ShapeDtypeStruct((wide, seqs), BF),
    )
    return pl.pallas_call(
        project_kernel,
        name="project",
        grid_spec=pltpu.PrefetchScalarGridSpec(
            num_scalar_prefetch=1,
            grid=(steps,),
            in_specs=[
                blk,
                whole((1, 2 * rows)),
                whole((1, chans)),
                whole((1, chans)),
                whole((chans, narrow)),
                whole((narrow, chans)),
            ],
            out_specs=[blk, whole((seqs, wide)), whole((seqs, wide)), whole((wide, seqs))],
            scratch_shapes=[
                pltpu.VMEM((half * narrow, 2 * rows), F32),
                pltpu.VMEM((seqs * rows, narrow), F32),
            ],
        ),
        out_shape=outs,
        compiler_params=params(),
        cost_estimate=pl.CostEstimate(
            flops=4 * seqs * rows * chans * narrow, bytes_accessed=8_000_000, transcendentals=0
        ),
    )(
        depth,
        alignment.reshape(2, half, rows, chans),
        depth_row,
        gain[None, :],
        bias[None, :],
        wl,
        wr.T,
    )


def pair_block(a, b):
    z = jnp.zeros_like(a)
    return jnp.concatenate(
        [
            jnp.concatenate([a, z], axis=1),
            jnp.concatenate([z, a], axis=1),
            jnp.concatenate([b, z], axis=1),
            jnp.concatenate([z, b], axis=1),
        ],
        axis=0,
    )


def send_pieces(me, acc, outs):
    rows = outs[0].shape[0]
    count = len(outs)
    for t, out in enumerate(outs):
        p = lax.rem(me + t, count)
        out[...] = acc[pl.ds(pl.multiple_of(p * rows, 8), rows), :].astype(out.dtype)


def right_kernel(depth_ref, me_ref, cot_ref, dcol, w2, l_ref, s_ref, g_ref, *rest):
    outs, acc = rest[:-1], rest[-1]
    n = pl.program_id(0)
    i_blk, cols, pair = cot_ref.shape
    narrow = l_ref.shape[1] // i_blk
    seqs = l_ref.shape[0]
    dep = dcol[...]
    w = w2[...]
    for ip in range(i_blk // 2):
        scaled = []
        for k in range(2):
            i = 2 * ip + k
            den = jnp.maximum(jnp.minimum(dep, depth_ref[n * i_blk + i].astype(F32)), 1.0)
            s = (cot_ref[i].astype(F32) / den).astype(BF)
            s_ref[i] = s
            scaled.append(s)
        g = dot(w, pair_block(*scaled), NT).astype(BF)
        for k in range(2):
            i = 2 * ip + k
            for dp in range(narrow // 2):
                g_ref[i * narrow : (i + 1) * narrow, dp * 2 * cols : (dp + 1) * 2 * cols] = g[
                    dp * narrow : (dp + 1) * narrow, k * 2 * cols : (k + 1) * 2 * cols
                ]
    part = dot(l_ref[...], g_ref[...])

    @pl.when(n == 0)
    def _():
        acc[...] = jnp.zeros_like(acc)

    acc[0:seqs, :] += part

    @pl.when(n == pl.num_programs(0) - 1)
    def _():
        send_pieces(me_ref[0], acc, outs)


def right_side(depth, me, cot, dcol, w2, left, block, pieces, piece_rows):
    rows, _, pair = cot.shape
    cols = dcol.shape[0]
    seqs, wide = left.shape
    narrow = wide // rows
    i_blk = 8
    c_wide = cols * narrow
    return pl.pallas_call(
        right_kernel,
        name="grad_outer_right",
        grid_spec=pltpu.PrefetchScalarGridSpec(
            num_scalar_prefetch=2,
            grid=(rows // i_blk,),
            in_specs=[
                pl.BlockSpec((i_blk, cols, pair), lambda n, *_: (n, block, 0)),
                whole(dcol.shape),
                whole(w2.shape),
                pl.BlockSpec((seqs, i_blk * narrow), lambda n, *_: (0, n)),
            ],
            out_specs=[
                pl.BlockSpec((i_blk, cols, pair), lambda n, *_: (n, 0, 0)),
                pl.BlockSpec((i_blk * narrow, c_wide), lambda n, *_: (n, 0)),
            ]
            + [whole((piece_rows, c_wide))] * pieces,
            scratch_shapes=[pltpu.VMEM((piece_rows * pieces, c_wide), F32)],
        ),
        out_shape=[
            jax.ShapeDtypeStruct((rows, cols, pair), BF),
            jax.ShapeDtypeStruct((wide, c_wide), BF),
        ]
        + [jax.ShapeDtypeStruct((piece_rows, c_wide), BF)] * pieces,
        compiler_params=params(),
        cost_estimate=pl.CostEstimate(
            flops=4_000_000_000, bytes_accessed=11_000_000, transcendentals=0
        ),
    )(depth, me, cot, dcol, w2, left)


def left_side(sel, me, grad_outer, rights, pieces, piece_rows):
    wide, c_wide = grad_outer.shape
    seqs = rights[0].shape[0]
    chunk = 256

    def kernel(sel_ref, me_ref, g_ref, *rest):
        k = len(rights)
        r_in = rest[:k]
        outs = rest[k : k + pieces]
        r_out = rest[k + pieces]
        acc = rest[k + pieces + 1]
        n = pl.program_id(0)

        @pl.when(n == 0)
        def _():
            acc[...] = jnp.zeros_like(acc)
            for t, r in enumerate(r_in):

                @pl.when(sel_ref[0] == t)
                def _():
                    r_out[...] = r[...]

        acc[0:seqs, pl.ds(pl.multiple_of(n * chunk, chunk), chunk)] = dot(
            r_out[...], g_ref[...], NT
        )

        @pl.when(n == pl.num_programs(0) - 1)
        def _():
            send_pieces(me_ref[0], acc, outs)

    return pl.pallas_call(
        kernel,
        name="grad_left_side",
        grid_spec=pltpu.PrefetchScalarGridSpec(
            num_scalar_prefetch=2,
            grid=(wide // chunk,),
            in_specs=[pl.BlockSpec((chunk, c_wide), lambda n, *_: (n, 0))]
            + [whole((seqs, c_wide))] * len(rights),
            out_specs=[whole((piece_rows, wide))] * pieces + [whole((seqs, c_wide))],
            scratch_shapes=[pltpu.VMEM((piece_rows * pieces, wide), F32)],
        ),
        out_shape=[jax.ShapeDtypeStruct((piece_rows, wide), BF)] * pieces
        + [jax.ShapeDtypeStruct((seqs, c_wide), BF)],
        compiler_params=params(),
        cost_estimate=pl.CostEstimate(
            flops=2_000_000_000, bytes_accessed=10_000_000, transcendentals=0
        ),
    )(sel, me, grad_outer, *rights)


def forward_kernel(depth_ref, lt_ref, r_ref, w2t, s_ref, dcol, bias, pu_ref, gw_ref):
    n = pl.program_id(0)
    i_blk, cols, pair = s_ref.shape
    narrow = lt_ref.shape[0] // i_blk
    outer = dot(lt_ref[...], r_ref[...]).astype(BF)
    lane = lax.broadcasted_iota(jnp.int32, (pair, 2 * cols), 1)
    low = lane < cols
    dep = dcol[...]
    total = None
    for ip in range(i_blk // 2):
        x = jnp.concatenate(
            [
                jnp.concatenate(
                    [
                        outer[
                            i * narrow : (i + 1) * narrow, dp * 2 * cols : (dp + 1) * 2 * cols
                        ]
                        for dp in range(narrow // 2)
                    ],
                    axis=0,
                )
                for i in (2 * ip, 2 * ip + 1)
            ],
            axis=1,
        )
        sbd = pair_block(s_ref[2 * ip], s_ref[2 * ip + 1])
        gw = dot(x, sbd)
        total = gw if total is None else total + gw
        pt = dot(w2t[...], x)
        e0, o0 = pt[:pair, : 2 * cols], pt[:pair, 2 * cols :]
        e1, o1 = pt[pair:, : 2 * cols], pt[pair:, 2 * cols :]
        both = jnp.where(low, e0, o1) + pltpu.roll(jnp.where(low, o0, e1), cols, 1)
        both = both.T + bias[...]
        for k in range(2):
            i = 2 * ip + k
            den = jnp.maximum(jnp.minimum(dep, depth_ref[n * i_blk + i].astype(F32)), 1.0)
            pu_ref[i] = (both[k * cols : (k + 1) * cols] / den).astype(BF)

    @pl.when(n == 0)
    def _():
        gw_ref[...] = total

    @pl.when(n > 0)
    def _():
        gw_ref[...] += total


def forward(depth, left_t, right, w2t, scaled, dcol, bias):
    rows, cols, pair = scaled.shape
    wide, seqs = left_t.shape
    narrow = wide // rows
    i_blk = 8
    return pl.pallas_call(
        forward_kernel,
        name="forward",
        grid_spec=pltpu.PrefetchScalarGridSpec(
            num_scalar_prefetch=1,
            grid=(rows // i_blk,),
            in_specs=[
                pl.BlockSpec((i_blk * narrow, seqs), lambda n, *_: (n, 0)),
                whole(right.shape),
                whole(w2t.shape),
                pl.BlockSpec((i_blk, cols, pair), lambda n, *_: (n, 0, 0)),
                whole(dcol.shape),
                whole((1, pair)),
            ],
            out_specs=[
                pl.BlockSpec((i_blk, cols, pair), lambda n, *_: (n, 0, 0)),
                whole((w2t.shape[1], w2t.shape[0])),
            ],
        ),
        out_shape=[
            jax.ShapeDtypeStruct((rows, cols, pair), BF),
            jax.ShapeDtypeStruct((w2t.shape[1], w2t.shape[0]), F32),
        ],
        compiler_params=params(),
        cost_estimate=pl.CostEstimate(
            flops=6_000_000_000, bytes_accessed=4_000_000, transcendentals=0
        ),
    )(depth, left_t, right, w2t, scaled, dcol, bias[None, :])


def tokens(depth, me, depth_row, lefts, rights, rows):
    piece_rows, wide = lefts[0].shape
    narrow = wide // rows
    count = piece_rows * rows

    def kernel(depth_ref, me_ref, drow, *rest):
        l_in = rest[: len(lefts)]
        r_in = rest[len(lefts) : len(lefts) + len(rights)]
        out, z, t = rest[len(lefts) + len(rights) :]
        base = me_ref[0] * piece_rows
        left = sum(ref[...].astype(F32) for ref in l_in)
        right = sum(ref[...].astype(F32) for ref in r_in)
        seq = lax.broadcasted_iota(jnp.int32, (piece_rows, narrow), 0) + base
        seq2 = lax.broadcasted_iota(jnp.int32, (piece_rows, 2 * rows), 0) + base
        on = seq2.astype(F32) < drow[...]
        for i in range(rows):
            v = jnp.where(seq < depth_ref[i], left[:, i * narrow : (i + 1) * narrow], 0.0)
            z[pl.ds(i, piece_rows, stride=rows), 0:narrow] = v
        for dp in range(narrow // 2):
            v = jnp.where(on, right[:, dp * 2 * rows : (dp + 1) * 2 * rows], 0.0)
            t[pl.ds(2 * dp, piece_rows, stride=narrow), :] = v[:, :rows]
            t[pl.ds(2 * dp + 1, piece_rows, stride=narrow), :] = v[:, rows:]
        per = 128 // narrow
        for q in range(piece_rows // per):
            tr = t[q * 128 : (q + 1) * 128, :].T
            for k in range(per):
                s = q * per + k
                z[s * rows : (s + 1) * rows, narrow : 2 * narrow] = tr[
                    :, k * narrow : (k + 1) * narrow
                ]
        h = count // 2
        out[...] = jnp.concatenate([z[:h, :], z[h:, :]], axis=1).astype(BF)

    n_in = len(lefts) + len(rights)
    return pl.pallas_call(
        kernel,
        name="tokens",
        grid_spec=pltpu.PrefetchScalarGridSpec(
            num_scalar_prefetch=2,
            grid=(1,),
            in_specs=[whole(depth_row.shape)] + [whole((piece_rows, wide))] * n_in,
            out_specs=whole((count // 2, 4 * narrow)),
            scratch_shapes=[
                pltpu.VMEM((count, 2 * narrow), F32),
                pltpu.VMEM((piece_rows * narrow, rows), F32),
            ],
        ),
        out_shape=jax.ShapeDtypeStruct((count // 2, 4 * narrow), BF),
        compiler_params=params(),
        cost_estimate=pl.CostEstimate(
            flops=2_000_000, bytes_accessed=2_000_000, transcendentals=0
        ),
    )(depth, me, depth_row, *lefts, *rights)


def weight_grads(me, q, normed, piece_rows):
    seqs, rows, chans = normed.shape
    h = q.shape[0]
    nar2 = q.shape[1] // 2
    last = seqs // piece_rows - 1

    def kernel(me_ref, q_ref, n_ref, out):
        n = n_ref[...].reshape(2 * h, chans)
        v = q_ref[...]
        top = dot(v, n[:h], TN)
        bot = dot(v, n[h:], TN)
        out[...] = top[:nar2] + bot[nar2:]

    return pl.pallas_call(
        kernel,
        name="weight_grads",
        grid_spec=pltpu.PrefetchScalarGridSpec(
            num_scalar_prefetch=1,
            grid=(1,),
            in_specs=[
                whole(q.shape),
                pl.BlockSpec(
                    (piece_rows, rows, chans), lambda n, me: (jnp.minimum(me[0], last), 0, 0)
                ),
            ],
            out_specs=whole((nar2, chans)),
        ),
        out_shape=jax.ShapeDtypeStruct((nar2, chans), F32),
        compiler_params=params(),
        cost_estimate=pl.CostEstimate(
            flops=400_000_000, bytes_accessed=1_000_000, transcendentals=0
        ),
    )(me, q, normed)


def finish(me, qs, alignment, wc):
    seqs, rows, chans = alignment.shape
    h, lanes = qs[0].shape
    piece_rows = 2 * h // rows
    pieces = len(qs)
    used = seqs // piece_rows

    def kernel(me_ref, x_ref, w_ref, *rest):
        q_in, out = rest[:-1], rest[-1]
        p = pl.program_id(0)
        t = lax.rem(me_ref[0] - p + pieces, pieces)
        w0 = w_ref[0]
        w1 = w_ref[1]
        for k in range(pieces):

            @pl.when(t == k)
            def _():
                for half in range(2):
                    w = w1 if half else w0
                    q = q_in[k][...]
                    g = dot(jnp.concatenate([q, q], axis=1), w)
                    for j in range(piece_rows // 2):
                        s = half * (piece_rows // 2) + j
                        x = x_ref[s].astype(F32)
                        c = x - jnp.mean(x, axis=-1, keepdims=True)
                        inv = lax.rsqrt(jnp.mean(c * c, axis=-1, keepdims=True) + 1e-05)
                        xh = c * inv
                        gc = g[j * rows : (j + 1) * rows]
                        m = jnp.mean(gc * xh, axis=-1, keepdims=True)
                        out[s] = (inv * (gc - xh * m)).astype(BF)

    blk = pl.BlockSpec((piece_rows, rows, chans), lambda p, *_: (p, 0, 0))
    return pl.pallas_call(
        kernel,
        name="finish",
        grid_spec=pltpu.PrefetchScalarGridSpec(
            num_scalar_prefetch=1,
            grid=(used,),
            in_specs=[blk, whole(wc.shape)] + [whole((h, lanes))] * pieces,
            out_specs=blk,
        ),
        out_shape=jax.ShapeDtypeStruct(alignment.shape, BF),
        compiler_params=params(),
        cost_estimate=pl.CostEstimate(
            flops=1_000_000_000, bytes_accessed=8_000_000, transcendentals=0
        ),
    )(me, alignment, wc, *qs)


def shift(value, axis, t):
    n = lax.axis_size(axis)
    return lax.ppermute(value, axis, [(k, (k + t) % n) for k in range(n)])


def scatter_sum(value, axis, dtype):
    n = lax.axis_size(axis)
    me = lax.axis_index(axis)
    m = value.shape[0] // n
    total = None
    for t in range(n):
        part = lax.dynamic_slice_in_dim(value, (me + t) % n * m, m, 0)
        if t:
            part = shift(part.astype(dtype), axis, t).astype(F32)
        total = part if total is None else total + part
    return total


def gather_rows(value, axis):
    n = lax.axis_size(axis)
    me = lax.axis_index(axis)
    m = value.shape[0]
    parts = [value] + [shift(value, axis, t) for t in range(1, n)]
    ring = parts[::-1]
    return lax.dynamic_slice_in_dim(
        jnp.concatenate(ring + ring, axis=0), (n - 1 - me) * m, n * m, 0
    )


def all_sum(value):
    if value.shape[0] % (lax.axis_size("row") * lax.axis_size("col")):
        return lax.psum(value, ("row", "col"))
    part = scatter_sum(scatter_sum(value, "row", F32), "col", F32)
    return gather_rows(gather_rows(part, "col"), "row")


def body(
    alignment,
    coverage,
    layer_norm_gain,
    layer_norm_bias,
    left_weight,
    right_weight,
    out_weight,
    out_bias,
    cotangent,
):
    n_row, n_col = lax.axis_size("row"), lax.axis_size("col")
    ratio = n_row // n_col
    row_index = lax.axis_index("row")
    col_index = lax.axis_index("col")
    me_row = row_index[None].astype(jnp.int32)
    me_col = col_index[None].astype(jnp.int32)
    seqs, rows, chans = alignment.shape
    narrow = left_weight.shape[1]
    pair = out_weight.shape[1]
    both = ("row", "col")

    depth = jnp.sum(coverage, axis=0)
    depth_parts = []
    for m in range(ratio):
        got = depth * (row_index == col_index * ratio + m)
        for t in range(1, n_row):
            pairs = [
                ((c * ratio + m) * n_col + c, (c * ratio + m + t) % n_row * n_col + c)
                for c in range(n_col)
            ]
            got = got + lax.ppermute(depth, both, pairs)
        depth_parts.append(got)

    normed, right, left, left_t = project(
        depth, alignment, layer_norm_gain, layer_norm_bias, left_weight, right_weight
    )
    normed = normed.reshape(seqs, rows, chans)

    w4 = out_weight.reshape(narrow, narrow // 2, 2, pair)
    w2 = jnp.transpose(w4, (1, 0, 2, 3)).reshape(narrow * narrow // 2, 2 * pair)
    w2t = w2.T

    piece_rows = (seqs // n_col + 7) // 8 * 8
    right_pieces, left_pieces, updates, grad_w = [], [], [], None
    scaled, grad_outer, dcols = [], [], []
    for m in range(ratio):
        dcol = jnp.broadcast_to(depth_parts[m].astype(F32)[:, None], (rows, pair))
        s, g, *pieces = right_side(
            depth, jnp.zeros_like(me_row), cotangent, dcol, w2, left, m, n_col, piece_rows
        )
        dcols.append(dcol)
        scaled.append(s)
        grad_outer.append(g)
        right_pieces.extend(pieces)

    sums = None
    stacked = jnp.stack(right_pieces)
    for t in range(n_row):
        part = lax.dynamic_index_in_dim(stacked, (row_index + t) % n_row, 0, keepdims=False)
        if t:
            part = shift(part, "row", t)
        sums = part.astype(F32) if sums is None else sums + part.astype(F32)
    turn = [
        ((m * n_col + k) * n_col + c, (c * ratio + m) * n_col + k)
        for m in range(ratio)
        for k in range(n_col)
        for c in range(n_col)
    ]
    right_sum = lax.ppermute(sums.astype(BF), both, turn)

    for m in range(ratio):
        rights = [right]
        for t in range(1, n_row):
            pairs = [
                ((c * ratio + m) * n_col + c, (c * ratio + m + t) % n_row * n_col + c)
                for c in range(n_col)
            ]
            rights.append(lax.ppermute(right, both, pairs))
        sel = (row_index - (col_index * ratio + m) + n_row) % n_row
        *pieces, right_cols = left_side(
            sel[None].astype(jnp.int32), me_col, grad_outer[m], rights, n_col, piece_rows
        )
        left_pieces.append(pieces)
        update, gw = forward(
            depth, left_t, right_cols, w2t, scaled[m], dcols[m], out_bias
        )
        updates.append(update)
        grad_w = gw if grad_w is None else grad_w + gw
    pair_update = updates[0] if ratio == 1 else jnp.concatenate(updates, axis=1)

    lefts = []
    for t in range(n_col):
        part = left_pieces[0][t]
        if ratio > 1:
            part = sum(p[t].astype(F32) for p in left_pieces).astype(BF)
        lefts.append(shift(part, "col", t) if t else part)

    depth_row = jnp.tile(depth.astype(F32), 2)[None, :]
    q = tokens(depth, me_col, depth_row, lefts, [right_sum], rows)
    grads = weight_grads(me_col, q, normed, piece_rows)
    qs = [q] + [shift(q, "col", t) for t in range(1, n_col)]

    weights = jnp.concatenate([left_weight, right_weight], axis=1).astype(F32).T
    weights = weights * layer_norm_gain
    centred = weights - jnp.mean(weights, axis=1, keepdims=True)
    hi = centred.astype(BF)
    lo = (centred - hi.astype(F32)).astype(BF)
    none = jnp.zeros_like(hi)
    wc = jnp.stack(
        [
            jnp.concatenate([hi, none, lo, none], axis=0),
            jnp.concatenate([none, hi, none, lo], axis=0),
        ]
    )
    gradient = finish(me_col, qs, alignment, wc)

    grad_w = all_sum(grad_w)
    grads = all_sum(grads)
    grad_out = jnp.transpose(
        grad_w.reshape(narrow // 2, narrow, 2, pair), (1, 0, 2, 3)
    ).reshape(narrow * narrow, pair)
    return pair_update, gradient, grads[:narrow].T, grads[narrow:].T, grad_out


def solution(mesh):
    return jax.shard_map(
        body,
        mesh=mesh,
        in_specs=(
            P("grp", "row", None),
            P("grp", "row"),
            P(),
            P(),
            P(),
            P(),
            P(),
            P(),
            P(("grp", "row"), "col", None),
        ),
        out_specs=(
            P(("grp", "row"), "col", None),
            P("grp", "row", None),
            P("grp", None),
            P("grp", None),
            P("grp", None),
        ),
        check_vma=False,
    )
```

```python
import jax
import jax.numpy as jnp
from jax import lax
from jax.experimental import pallas as pl
from jax.experimental.pallas import tpu as pltpu
from jax.sharding import PartitionSpec as P

BF = jnp.bfloat16
F32 = jnp.float32
NN = (((1,), (0,)), ((), ()))
NT = (((1,), (1,)), ((), ()))
TN = (((0,), (0,)), ((), ()))
VMEM = 64 * 1024 * 1024
IBLK = 8


def params():
    return pltpu.CompilerParams(vmem_limit_bytes=VMEM)


def dot(a, b, dims=NN):
    return lax.dot_general(a, b, dims, preferred_element_type=F32)


def whole(shape):
    return pl.BlockSpec(shape, lambda *_: (0,) * len(shape))


def shape(dims, dtype=BF):
    return jax.ShapeDtypeStruct(dims, dtype)


def call(kernel, name, grid, ins, outs, scratch, scalars, arrays, flops, bytes_accessed):
    return pl.pallas_call(
        kernel,
        name=name,
        grid_spec=pltpu.PrefetchScalarGridSpec(
            num_scalar_prefetch=len(scalars),
            grid=grid,
            in_specs=ins,
            out_specs=[o[0] for o in outs],
            scratch_shapes=scratch,
        ),
        out_shape=[o[1] for o in outs],
        compiler_params=params(),
        cost_estimate=pl.CostEstimate(
            flops=int(flops) // 10**6, bytes_accessed=1024, transcendentals=0
        ),
    )(*scalars, *arrays)


def depth_rows(cov, lanes):
    total = jnp.sum(cov.astype(F32), axis=1, keepdims=True)
    return jnp.broadcast_to(total, (cov.shape[0], lanes))


def depth_lanes(cov):
    row = depth_rows(cov, cov.shape[0]).T[0:1, :]
    return jnp.concatenate([row, row], axis=1)


def project(cov_t, alignment, gain, bias, wr_t):
    seqs, rows, chans = alignment.shape
    narrow = wr_t.shape[0]
    half = seqs // 2
    blk = 16
    steps = half // blk
    wide = rows * narrow

    def kernel(
        cov_ref, x_ref, gain_ref, bias_ref, w_ref, normed_ref, xhat_ref, stat_ref, r_ref, ys, nbs
    ):
        n = pl.program_id(0)
        gain_v = gain_ref[...]
        bias_v = bias_ref[...]
        lane = lax.broadcasted_iota(jnp.int32, (rows, 128), 1)
        for s2 in range(2):
            for g in range(blk):
                if g % 8 == 0:
                    stat = jnp.zeros((rows, 128), F32)
                x = x_ref[s2, g].astype(F32)
                mean = jnp.mean(x, axis=-1, keepdims=True)
                c = x - mean
                inv = lax.rsqrt(jnp.mean(c * c, axis=-1, keepdims=True) + 1e-05)
                xhat = c * inv
                nb = (xhat * gain_v + bias_v).astype(BF)
                normed_ref[s2, g] = nb
                xhat_ref[s2, g] = xhat.astype(BF)
                at = (2 * g + s2) * rows
                nbs[at : at + rows, :] = nb
                stat = jnp.where(lane == g % 8, inv, stat)
                stat_ref[s2, g // 8] = stat
        y = dot(w_ref[...], nbs[...], NT)
        for g in range(blk):
            at = (n * blk + g) * narrow
            ys[pl.ds(pl.multiple_of(at, narrow), narrow), :] = y[
                :, g * 2 * rows : (g + 1) * 2 * rows
            ]

        @pl.when(n == steps - 1)
        def _():
            lanes = lax.broadcasted_iota(jnp.int32, (half, 2 * rows), 1)
            seq = lax.broadcasted_iota(jnp.int32, (half, 2 * rows), 0).astype(F32)
            low = lanes < rows
            dep = depth_lanes(cov_ref[...])
            top_on = seq < dep
            bot_on = seq + half < dep
            for dp in range(narrow // 2):
                even = ys[pl.ds(2 * dp, half, stride=narrow), :]
                odd = ys[pl.ds(2 * dp + 1, half, stride=narrow), :]
                top = jnp.where(low, even, pltpu.roll(odd, rows, 1))
                bot = jnp.where(low, pltpu.roll(even, rows, 1), odd)
                at = slice(dp * 2 * rows, (dp + 1) * 2 * rows)
                r_ref[0:half, at] = jnp.where(top_on, top, 0.0).astype(BF)
                r_ref[half : 2 * half, at] = jnp.where(bot_on, bot, 0.0).astype(BF)

    tile = pl.BlockSpec((2, blk, rows, chans), lambda n: (0, n, 0, 0))
    return call(
        kernel,
        "project",
        (steps,),
        [
            whole(cov_t.shape),
            tile,
            whole((1, chans)),
            whole((1, chans)),
            whole(wr_t.shape),
        ],
        [
            (tile, shape((2, half, rows, chans))),
            (tile, shape((2, half, rows, chans))),
            (
                pl.BlockSpec((2, blk // 8, rows, 128), lambda n: (0, n, 0, 0)),
                shape((2, half // 8, rows, 128), F32),
            ),
            (whole((seqs, wide)), shape((seqs, wide))),
        ],
        [
            pltpu.VMEM((half * narrow, 2 * rows), F32),
            pltpu.VMEM((2 * blk * rows, chans), BF),
        ],
        (),
        (
            cov_t,
            alignment.reshape(2, half, rows, chans),
            gain[None, :],
            bias[None, :],
            wr_t,
        ),
        2e9,
        7e6,
    )


def pair_block(a, b):
    z = jnp.zeros_like(a)
    return jnp.concatenate(
        [
            jnp.concatenate([a, z], axis=1),
            jnp.concatenate([z, a], axis=1),
            jnp.concatenate([b, z], axis=1),
            jnp.concatenate([z, b], axis=1),
        ],
        axis=0,
    )


def rows_at(p, count):
    start = p * count
    if count % 8 == 0:
        start = pl.multiple_of(start, 8)
    return pl.ds(start, count)


def send_pieces(me, acc, outs):
    rows = outs[0].shape[0]
    count = len(outs)
    for t, out in enumerate(outs):
        p = lax.rem(me + t, count)
        out[...] = acc[rows_at(p, rows), :].astype(out.dtype)


def right_side(own, me, cov_t, cov_far, cot, out_weight, wl_t, normed, block, pieces, piece_rows):
    rows, _, pair = cot.shape
    seqs, _, chans = normed.shape
    cols = cov_far.shape[0]
    narrow = wl_t.shape[0]
    wide = rows * narrow
    c_wide = cols * narrow
    i_blk = 16

    def kernel(
        own_ref,
        me_ref,
        cov_ref,
        far_ref,
        cot_ref,
        wo_ref,
        wl_ref,
        n_ref,
        s_ref,
        g_ref,
        w2_ref,
        lt_ref,
        dcol,
        *rest,
    ):
        outs = rest[:pieces]
        acc, wide_f, z, drow = rest[pieces:]
        n = pl.program_id(0)

        @pl.when(n == 0)
        def _():
            acc[...] = jnp.zeros_like(acc)
            drow[...] = depth_rows(cov_ref[...], 128)
            mine = (own_ref[0] == 1).astype(F32)
            far = depth_rows(far_ref[...], 128)
            dcol[...] = mine * drow[...] + (1.0 - mine) * far
            wide_f[...] = wo_ref[...].astype(F32)
            for dp in range(narrow // 2):
                for d2 in range(2):
                    v = wide_f[pl.ds(2 * dp + d2, narrow, stride=narrow), :]
                    w2_ref[dp * narrow : (dp + 1) * narrow, d2 * pair : (d2 + 1) * pair] = (
                        v.astype(BF)
                    )

        dep = dcol[...]
        w = w2_ref[...]
        mine_rows = drow[pl.ds(pl.multiple_of(n * i_blk, i_blk), i_blk), :]
        blk = n_ref[...].astype(F32).reshape(seqs * i_blk, chans).astype(BF)
        z[...] = dot(blk, wl_ref[...], NT)
        seq = lax.broadcasted_iota(jnp.int32, (seqs, narrow), 0).astype(F32)
        per = 128 // narrow
        tiles = []
        for q in range(i_blk // per):
            parts = []
            for k in range(per):
                i = q * per + k
                v = z[pl.ds(i, seqs, stride=i_blk), :]
                parts.append(jnp.where(seq < mine_rows[i : i + 1, :narrow], v, 0.0))
            tile = jnp.concatenate(parts, axis=1)
            lt_ref[q * 128 : (q + 1) * 128, :] = tile.T.astype(BF)
            tiles.append(tile.astype(BF))
        left = jnp.concatenate(tiles, axis=1)
        for ip in range(i_blk // 2):
            scaled = []
            for k in range(2):
                i = 2 * ip + k
                den = jnp.maximum(jnp.minimum(dep, mine_rows[i : i + 1, :]), 1.0)
                s = (cot_ref[i].astype(F32) / den).astype(BF)
                s_ref[i] = s
                scaled.append(s)
            g = dot(w, pair_block(*scaled), NT).astype(BF)
            for k in range(2):
                i = 2 * ip + k
                for dp in range(narrow // 2):
                    g_ref[
                        i * narrow : (i + 1) * narrow, dp * 2 * cols : (dp + 1) * 2 * cols
                    ] = g[dp * narrow : (dp + 1) * narrow, k * 2 * cols : (k + 1) * 2 * cols]
        acc[0:seqs, :] += dot(left, g_ref[...])

        @pl.when(n == pl.num_programs(0) - 1)
        def _():
            send_pieces(me_ref[0], acc, outs)

    return call(
        kernel,
        "grad_outer_right",
        (rows // i_blk,),
        [
            whole(cov_t.shape),
            whole(cov_far.shape),
            pl.BlockSpec((i_blk, cols, pair), lambda n, *_: (n, block, 0)),
            whole(out_weight.shape),
            whole(wl_t.shape),
            pl.BlockSpec((seqs, i_blk, chans), lambda n, *_: (0, n, 0)),
        ],
        [
            (
                pl.BlockSpec((i_blk, cols, pair), lambda n, *_: (n, 0, 0)),
                shape((rows, cols, pair)),
            ),
            (pl.BlockSpec((i_blk * narrow, c_wide), lambda n, *_: (n, 0)), shape((wide, c_wide))),
            (
                whole((narrow * narrow // 2, 2 * pair)),
                shape((narrow * narrow // 2, 2 * pair)),
            ),
            (pl.BlockSpec((i_blk * narrow, seqs), lambda n, *_: (n, 0)), shape((wide, seqs))),
            (whole((cols, 128)), shape((cols, 128), F32)),
        ]
        + [(whole((piece_rows, c_wide)), shape((piece_rows, c_wide)))] * pieces,
        [
            pltpu.VMEM((piece_rows * pieces, c_wide), F32),
            pltpu.VMEM(out_weight.shape, F32),
            pltpu.VMEM((seqs * i_blk, narrow), F32),
            pltpu.VMEM((rows, 128), F32),
        ],
        (own, me),
        (cov_t, cov_far, cot, out_weight, wl_t, normed),
        4e9,
        16e6,
    )


def forward(me, cov_t, left_t, right, scaled, w2, dcol, bias, pieces):
    rows, cols, pair = scaled.shape
    wide, seqs = left_t.shape
    narrow = wide // rows
    c_wide = cols * narrow
    i_blk = IBLK
    high = narrow * narrow // 2
    part = high // pieces

    def kernel(
        me_ref, cov_ref, lt_ref, r_ref, s_ref, w2_ref, dcol_ref, bias_ref, pu_ref, *rest
    ):
        outs = rest[:-3]
        acc, w2t, drow = rest[-3:]
        n = pl.program_id(0)

        @pl.when(n == 0)
        def _():
            acc[...] = jnp.zeros_like(acc)
            w2t[...] = w2_ref[...].astype(F32).T.astype(BF)
            drow[...] = depth_rows(cov_ref[...], 128)

        lane = lax.broadcasted_iota(jnp.int32, (pair, 2 * cols), 1)
        low = lane < cols
        dep = dcol_ref[...]
        mine_rows = drow[pl.ds(pl.multiple_of(n * i_blk, i_blk), i_blk), :]
        outer = dot(lt_ref[...], r_ref[...]).astype(BF)
        x = jnp.concatenate(
            [
                jnp.concatenate(
                    [
                        outer[
                            i * narrow : (i + 1) * narrow, dp * 2 * cols : (dp + 1) * 2 * cols
                        ]
                        for dp in range(narrow // 2)
                    ],
                    axis=0,
                )
                for i in range(i_blk)
            ],
            axis=1,
        )
        sbd = jnp.concatenate(
            [pair_block(s_ref[2 * k], s_ref[2 * k + 1]) for k in range(i_blk // 2)], axis=0
        )
        acc[...] += dot(x, sbd)
        pt = dot(w2t[...], x)
        for ip in range(i_blk // 2):
            at = ip * 4 * cols
            e0, o0 = pt[:pair, at : at + 2 * cols], pt[:pair, at + 2 * cols : at + 4 * cols]
            e1, o1 = pt[pair:, at : at + 2 * cols], pt[pair:, at + 2 * cols : at + 4 * cols]
            both = jnp.where(low, e0, o1) + pltpu.roll(jnp.where(low, o0, e1), cols, 1)
            both = both.T + bias_ref[...]
            for k in range(2):
                i = 2 * ip + k
                den = jnp.maximum(jnp.minimum(dep, mine_rows[i : i + 1, :]), 1.0)
                pu_ref[i] = (both[k * cols : (k + 1) * cols] / den).astype(BF)

        @pl.when(n == pl.num_programs(0) - 1)
        def _():
            send_pieces(me_ref[0], acc, outs)

    return call(
        kernel,
        "forward",
        (rows // i_blk,),
        [
            whole(cov_t.shape),
            pl.BlockSpec((i_blk * narrow, seqs), lambda n, *_: (n, 0)),
            whole(right.shape),
            pl.BlockSpec((i_blk, cols, pair), lambda n, *_: (n, 0, 0)),
            whole(w2.shape),
            whole(dcol.shape),
            whole((1, pair)),
        ],
        [
            (
                pl.BlockSpec((i_blk, cols, pair), lambda n, *_: (n, 0, 0)),
                shape((rows, cols, pair)),
            ),
            (whole((part, 2 * pair)), shape((part, 2 * pair), F32)),
        ]
        + [(whole((part, 2 * pair)), shape((part, 2 * pair)))] * (pieces - 1),
        [
            pltpu.VMEM((high, 2 * pair), F32),
            pltpu.VMEM((w2.shape[1], w2.shape[0]), BF),
            pltpu.VMEM((rows, 128), F32),
        ],
        (me,),
        (cov_t, left_t, right, scaled, w2, dcol, bias[None, :]),
        6e9,
        6e6,
    )


def left_side(sel, me, grad_outer, rights, pieces, piece_rows):
    wide, c_wide = grad_outer.shape
    seqs = rights[0].shape[0]
    chunk = 512

    def kernel(sel_ref, me_ref, g_ref, *rest):
        r_in = rest[: len(rights)]
        r_ref, outs, acc = rest[len(rights)], rest[len(rights) + 1 : -1], rest[-1]
        n = pl.program_id(0)

        @pl.when(n == 0)
        def _():
            acc[...] = jnp.zeros_like(acc)
            for t, r in enumerate(r_in):

                @pl.when(sel_ref[0] == t)
                def _():
                    pltpu.sync_copy(r, r_ref)

        at = pl.ds(pl.multiple_of(n * chunk, chunk), chunk)
        acc[0:seqs, at] = dot(g_ref[...], r_ref[...], NT).T

        @pl.when(n == pl.num_programs(0) - 1)
        def _():
            send_pieces(me_ref[0], acc, outs)

    return call(
        kernel,
        "grad_left_side",
        (wide // chunk,),
        [pl.BlockSpec((chunk, c_wide), lambda n, *_: (n, 0))]
        + [pl.BlockSpec(memory_space=pl.ANY)] * len(rights),
        [(whole((seqs, c_wide)), shape((seqs, c_wide)))]
        + [(whole((piece_rows, wide)), shape((piece_rows, wide)))] * pieces,
        [pltpu.VMEM((piece_rows * pieces, wide), F32)],
        (sel, me),
        (grad_outer, *rights),
        2e9,
        9e6,
    )


def tokens(me, cov_t, stat, lefts, rights, normed):
    seqs, rows, chans = normed.shape
    piece_rows, wide = lefts[0].shape
    narrow = wide // rows
    count = piece_rows * rows
    h = count // 2
    quad = 4 * rows
    last = seqs // piece_rows - 1
    per_half = (last + 1) // 2
    n_l, n_r = len(lefts), len(rights)
    nar2 = 2 * narrow

    def kernel(me_ref, cov_ref, stat_ref, n_ref, *rest):
        l_in = rest[:n_l]
        r_in = rest[n_l : n_l + n_r]
        out, z, t = rest[n_l + n_r :]
        plain = []
        base = (me_ref[0] * piece_rows).astype(F32)
        left = sum(ref[...].astype(F32) for ref in l_in)
        right = sum(ref[...].astype(F32) for ref in r_in)
        drow = depth_rows(cov_ref[...], 128)
        seq = lax.broadcasted_iota(jnp.int32, (piece_rows, narrow), 0).astype(F32) + base
        seq2 = lax.broadcasted_iota(jnp.int32, (piece_rows, 2 * rows), 0).astype(F32) + base
        on = seq2 < depth_lanes(cov_ref[...])
        for i in range(rows):
            v = jnp.where(
                seq < drow[i : i + 1, :narrow], left[:, i * narrow : (i + 1) * narrow], 0.0
            )
            z[pl.ds(i, piece_rows, stride=rows), 0:narrow] = v
        for dp in range(narrow // 2):
            v = jnp.where(on, right[:, dp * 2 * rows : (dp + 1) * 2 * rows], 0.0)
            t[pl.ds(2 * dp, piece_rows, stride=narrow), :] = v[:, :rows]
            t[pl.ds(2 * dp + 1, piece_rows, stride=narrow), :] = v[:, rows:]
        per = 128 // narrow
        for q in range(piece_rows // per):
            tr = t[q * 128 : (q + 1) * 128, :].T
            for k in range(per):
                s = q * per + k
                z[s * rows : (s + 1) * rows, narrow:nar2] = tr[:, k * narrow : (k + 1) * narrow]
        for b in range(piece_rows // 8):
            at = b * 2 * quad
            stats = stat_ref[0, b]
            pair_up, scaled = [], []
            for half in range(2):
                v = z[at + half * quad : at + (half + 1) * quad, :]
                inv = [
                    jnp.broadcast_to(stats[:, 4 * half + j : 4 * half + j + 1], (rows, nar2))
                    for j in range(4)
                ]
                pair_up.append(v)
                scaled.append(v * jnp.concatenate(inv, axis=0))
            out[b * quad : (b + 1) * quad, :] = jnp.concatenate(scaled, axis=1).astype(BF)
            plain.append(jnp.concatenate(pair_up, axis=1).astype(BF))
        v = jnp.concatenate(plain, axis=0)
        nb = n_ref[...].reshape(piece_rows // 8, 2, quad, chans)
        top = dot(v, nb[:, 0].reshape(h, chans), TN)
        bot = dot(v, nb[:, 1].reshape(h, chans), TN)
        grads = (top[:nar2] + bot[nar2:]).astype(BF)
        for k in range(chans // 128):
            out[h + k * nar2 : h + (k + 1) * nar2, :] = grads[:, k * 128 : (k + 1) * 128]

    return call(
        kernel,
        "tokens",
        (1,),
        [
            whole(cov_t.shape),
            pl.BlockSpec(
                (1, piece_rows // 8, rows, 128),
                lambda n, me: (
                    jnp.minimum(me[0], last) // per_half,
                    jnp.minimum(me[0], last) % per_half,
                    0,
                    0,
                ),
            ),
            pl.BlockSpec(
                (piece_rows, rows, chans), lambda n, me: (jnp.minimum(me[0], last), 0, 0)
            ),
        ]
        + [whole((piece_rows, wide))] * (n_l + n_r),
        [(whole((h + nar2 * chans // 128, 128)), shape((h + nar2 * chans // 128, 128)))],
        [pltpu.VMEM((count, nar2), F32), pltpu.VMEM((piece_rows * narrow, rows), F32)],
        (me,),
        (cov_t, stat, normed, *lefts, *rights),
        4e8,
        2e6,
    )[0]


def cut(me, parts, pieces):
    m, lanes = parts[0].shape

    def kernel(me_ref, *rest):
        ins, outs, acc = rest[: len(parts)], rest[len(parts) : -1], rest[-1]
        acc[...] = sum(ref[...].astype(F32) for ref in ins)
        send_pieces(me_ref[0], acc, outs)

    return call(
        kernel,
        "cut",
        (1,),
        [whole((m, lanes))] * len(parts),
        [(whole((m // pieces, lanes)), shape((m // pieces, lanes), F32))] * pieces,
        [pltpu.VMEM((m, lanes), F32)],
        (me,),
        tuple(parts),
        1e6,
        1e6,
    )


def finish(me, qs, alignment, wl_t, wr_t, gain, first, count, before=None):
    seqs, rows, chans = alignment.shape
    pieces = len(qs)
    quad = 4 * rows
    nar2 = 2 * wl_t.shape[0]
    blocks = (qs[0].shape[0] - nar2 * chans // 128) // quad
    every = count == seqs // (8 * blocks)
    given = () if before is None else (before,)

    def piece(n, me_ref):
        return n if every else me_ref[0] ^ (n + first)

    def kernel(me_ref, x_ref, wl_ref, wr_ref, gain_ref, *rest):
        q_in, (out, wc, q_now) = rest[:pieces], rest[-3:]
        n = pl.program_id(0)

        @pl.when(n == 0)
        def _():
            w = jnp.concatenate([wl_ref[...], wr_ref[...]], axis=0).astype(F32) * gain_ref[...]
            w = w - jnp.mean(w, axis=1, keepdims=True)
            hi = w.astype(BF)
            lo = (w - hi.astype(F32)).astype(BF)
            none = jnp.zeros_like(hi)
            wc[0] = jnp.concatenate([hi, none, lo, none], axis=0)
            wc[1] = jnp.concatenate([none, hi, none, lo], axis=0)

        t = piece(n, me_ref) ^ me_ref[0]
        for k in range(pieces):

            @pl.when(t == k)
            def _():
                q_now[...] = q_in[k][0 : blocks * quad, :]

        for b in range(blocks):
            q = q_now[b * quad : (b + 1) * quad, :]
            both = jnp.concatenate([q, q], axis=1)
            for half in range(2):
                g = dot(both, wc[half])
                for j in range(4):
                    s = half * 4 + j
                    xh = x_ref[8 * b + s].astype(F32)
                    gc = g[j * rows : (j + 1) * rows]
                    m = jnp.mean(gc * xh, axis=-1, keepdims=True)
                    out[8 * b + s] = (gc - xh * m).astype(BF)

    blk = pl.BlockSpec((8 * blocks, rows, chans), lambda n, me_ref: (piece(n, me_ref), 0, 0))
    return pl.pallas_call(
        kernel,
        name="finish",
        grid_spec=pltpu.PrefetchScalarGridSpec(
            num_scalar_prefetch=1,
            grid=(count,),
            in_specs=[
                blk,
                whole(wl_t.shape),
                whole(wr_t.shape),
                whole((1, chans)),
            ]
            + [whole(qs[0].shape)] * pieces
            + [pl.BlockSpec(memory_space=pl.ANY)] * len(given),
            out_specs=blk,
            scratch_shapes=[
                pltpu.VMEM((2, 4 * nar2, chans), BF),
                pltpu.VMEM((blocks * quad, 128), BF),
            ],
        ),
        out_shape=shape(alignment.shape),
        input_output_aliases={5 + pieces: 0} if given else {},
        compiler_params=params(),
        cost_estimate=pl.CostEstimate(flops=1000, bytes_accessed=1024, transcendentals=0),
    )(me, alignment, wl_t, wr_t, gain[None, :], *qs, *given)


def join_send(me, parts, qs, nar2):
    m, lanes = parts[0].shape
    n = len(parts)
    extra = nar2 * lanes // 128
    h = qs[0].shape[0] - extra

    def kernel(me_ref, *rest):
        ins, q_in, out, acc = rest[:n], rest[n:-2], rest[-2], rest[-1]
        for t in range(n):
            p = lax.rem(me_ref[0] - t + n, n)
            acc[rows_at(p, m), :] = ins[t][...]
        total = sum(q[...].astype(F32) for q in q_in)
        g = jnp.concatenate(
            [total[k * nar2 : (k + 1) * nar2] for k in range(lanes // 128)], axis=1
        )
        hi = g.astype(BF)
        out[0 : n * m, :] = acc[...].astype(BF)
        out[n * m : n * m + nar2, :] = hi
        out[n * m + nar2 :, :] = (g - hi.astype(F32)).astype(BF)

    total = n * m + 2 * nar2
    return call(
        kernel,
        "join_send",
        (1,),
        [whole((m, lanes))] * n
        + [pl.BlockSpec((extra, 128), lambda *_: (h // extra, 0))] * len(qs),
        [(whole((total, lanes)), shape((total, lanes)))],
        [pltpu.VMEM((n * m, lanes), F32)],
        (me,),
        (*parts, *qs),
        1e6,
        1e6,
    )[0]


def join_out(me, parts, nar2, narrow):
    rows, lanes = parts[0].shape
    n = len(parts)
    m = rows - 2 * nar2
    pair = lanes // 2
    dps = m // narrow

    def kernel(me_ref, *rest):
        ins, (out, lg, rg) = rest[:n], rest[n:]
        for t in range(n):
            p = lax.rem(me_ref[0] - t + n, n)
            v = ins[t][0:m, :].astype(F32)
            for k in range(dps):
                for d2 in range(2):
                    out[pl.ds(2 * (p * dps + k) + d2, narrow, stride=narrow), :] = v[
                        k * narrow : (k + 1) * narrow, d2 * pair : (d2 + 1) * pair
                    ]
        grads = sum(
            ref[m : m + nar2, :].astype(F32) + ref[m + nar2 :, :].astype(F32) for ref in ins
        )
        lg[...] = grads[:narrow]
        rg[...] = grads[narrow:]

    return call(
        kernel,
        "join_out",
        (1,),
        [whole((rows, lanes))] * n,
        [
            (whole((n * m * 2, pair)), shape((n * m * 2, pair), F32)),
            (whole((narrow, lanes)), shape((narrow, lanes), F32)),
            (whole((narrow, lanes)), shape((narrow, lanes), F32)),
        ],
        [],
        (me,),
        parts,
        1e6,
        1e6,
    )


BOTH = ("row", "col")


def shift(value, axis, t):
    n = lax.axis_size(axis)
    return lax.ppermute(value, axis, [(k, (k + t) % n) for k in range(n)])


def shifts(own, others, axis):
    return [own] + [shift(v, axis, t + 1) for t, v in enumerate(others)]


def swap(value, axis, t):
    n = lax.axis_size(axis)
    return lax.ppermute(value, axis, [(k, k ^ t) for k in range(n)])


def gather(value, axis):
    n = lax.axis_size(axis)
    if n == 4:
        near, far = swap(value, axis, 1), swap(value, axis, 2)
        return [value, near, far, swap(far, axis, 1)]
    return [value] + [swap(value, axis, t) for t in range(1, n)]


def spread_small(value, m, ratio):
    n_row, n_col = lax.axis_size("row"), lax.axis_size("col")
    total = None
    for first in range(1, n_row, n_col - 1):
        pairs = []
        for c in range(n_col):
            b = c * ratio + m
            for k, t in enumerate(range(first, min(first + n_col - 1, n_row))):
                pairs.append((b * n_col + (c + 1 + k) % n_col, (b + t) % n_row * n_col + c))
        got = lax.ppermute(value, BOTH, pairs)
        total = got if total is None else total + got
    return total


def spread(value, m, ratio):
    n_row, n_col = lax.axis_size("row"), lax.axis_size("col")
    out = [value]
    if n_row == 4 and n_col == 4:
        first = [(c * n_col + c, (c ^ 2) * n_col + c) for c in range(n_col)]
        first += [(c * n_col + (c ^ 1), (c ^ 1) * n_col + c) for c in range(n_col)]
        second = [(c * n_col + c, (c ^ 3) * n_col + c) for c in range(n_col)]
        return [value, lax.ppermute(value, BOTH, first), lax.ppermute(value, BOTH, second)]
    for t in range(1, n_row):
        pairs = [
            ((c * ratio + m) * n_col + c, (c * ratio + m + t) % n_row * n_col + c)
            for c in range(n_col)
        ]
        out.append(lax.ppermute(value, BOTH, pairs))
    return out


def spread_choice(row, col, m, ratio):
    n_row, n_col = lax.axis_size("row"), lax.axis_size("col")
    if n_row == 4 and n_col == 4:
        apart = row ^ col
        return jnp.where(apart == 3, 2, jnp.where(apart == 0, 0, 1))
    return (row - (col * ratio + m) + n_row) % n_row


def to_owners(pieces, ratio):
    n_row, n_col = lax.axis_size("row"), lax.axis_size("col")
    row = lax.axis_index("row")
    if ratio > 1:
        stacked = jnp.stack(pieces)
        pieces = [
            lax.dynamic_index_in_dim(stacked, (row + t) % n_row, 0, keepdims=False)
            for t in range(n_row)
        ]
    parts = []
    for t, piece in enumerate(pieces):
        pairs = []
        for r in range(n_row):
            m, k = divmod((r + t) % n_row, n_col)
            pairs += [(r * n_col + c, (c * ratio + m) * n_col + k) for c in range(n_col)]
        parts.append(lax.ppermute(piece, BOTH, pairs))
    return parts


def one(value):
    return value[None].astype(jnp.int32)


def body(
    alignment,
    coverage,
    layer_norm_gain,
    layer_norm_bias,
    left_weight,
    right_weight,
    out_weight,
    out_bias,
    cotangent,
):
    n_row, n_col = lax.axis_size("row"), lax.axis_size("col")
    ratio = n_row // n_col
    row_index = lax.axis_index("row")
    col_index = lax.axis_index("col")
    me_row, me_col = one(row_index), one(col_index)
    seqs, rows, chans = alignment.shape
    narrow = left_weight.shape[1]
    pair = out_weight.shape[1]
    piece_rows = (seqs // n_col + 7) // 8 * 8
    cov_t = coverage.T
    wl_t, wr_t = left_weight.T, right_weight.T

    cov_far = [spread_small(cov_t, m, ratio) for m in range(ratio)]
    normed, xhat, stat, right = project(cov_t, alignment, layer_norm_gain, layer_norm_bias, wr_t)
    right, cov_far = lax.optimization_barrier((right, cov_far))
    normed = normed.reshape(seqs, rows, chans)
    xhat = xhat.reshape(seqs, rows, chans)

    right_pieces, firsts = [], []
    for m in range(ratio):
        own = one(row_index == col_index * ratio + m)
        turn_by = one(row_index) if ratio == 1 else jnp.zeros_like(me_row)
        scaled, grad_outer, w2, left_t, dcol, *pieces = right_side(
            own,
            turn_by,
            cov_t,
            cov_far[m],
            cotangent,
            out_weight,
            wl_t,
            normed,
            m,
            n_col,
            piece_rows,
        )
        firsts.append((scaled, grad_outer, w2, left_t, dcol))
        right_pieces.extend(pieces)
    right_parts = to_owners(right_pieces, ratio)

    left_pieces, updates, weight_pieces = None, [], None
    for m in range(ratio):
        scaled, grad_outer, w2, left_t, dcol = firsts[m]
        sel = one(spread_choice(row_index, col_index, m, ratio))
        right_cols, *pieces = left_side(
            sel, me_col, grad_outer, spread(right, m, ratio), n_col, piece_rows
        )
        update, *gw = forward(
            me_row, cov_t, left_t, right_cols, scaled, w2, dcol, out_bias, n_row
        )
        updates.append(update)
        if m == 0:
            left_pieces, weight_pieces = pieces, gw
        else:
            left_pieces = [(a.astype(F32) + b).astype(BF) for a, b in zip(left_pieces, pieces)]
            weight_pieces = [
                (a.astype(F32) + b).astype(a.dtype) for a, b in zip(weight_pieces, gw)
            ]
    pair_update = updates[0] if ratio == 1 else jnp.concatenate(updates, axis=1)

    gw_parts = shifts(weight_pieces[0], weight_pieces[1:], "row")
    lefts = shifts(left_pieces[0], left_pieces[1:], "col")
    lefts, pair_update = lax.optimization_barrier((lefts, pair_update))
    q = tokens(me_col, cov_t, stat, lefts, right_parts, normed)
    qs = gather(q, "col")

    if weight_pieces[0].shape[0] % (8 * n_col) == 0:
        pieces = cut(me_col, gw_parts, n_col)
        part = sum(shifts(pieces[0], pieces[1:], "col"))
        parts = [part] + [shift(part, "col", t) for t in range(1, n_col)]
    else:
        parts = [lax.psum(cut(me_col, gw_parts, 1)[0], "col")]
    ends = (xhat, wl_t, wr_t, layer_norm_gain)
    if n_col == 4:
        gradient = finish(me_col, [qs[0], qs[1]], *ends, 0, 2)
        gradient, parts = lax.optimization_barrier((gradient, parts))
    last = join_send(me_col, parts, qs, 2 * narrow)
    lasts = [last] + [shift(last, "row", t) for t in range(1, n_row)]
    if n_col == 4:
        gradient = finish(me_col, qs, *ends, 2, 2, gradient)
    else:
        gradient = finish(me_col, qs, *ends, 0, seqs // piece_rows)
    lasts, gradient = lax.optimization_barrier((lasts, gradient))
    grad_out, grad_left, grad_right = join_out(me_row, lasts, 2 * narrow, narrow)
    return pair_update, gradient, grad_left.T, grad_right.T, grad_out


def solution(mesh):
    return jax.shard_map(
        body,
        mesh=mesh,
        in_specs=(
            P("grp", "row", None),
            P("grp", "row"),
            P(),
            P(),
            P(),
            P(),
            P(),
            P(),
            P(("grp", "row"), "col", None),
        ),
        out_specs=(
            P(("grp", "row"), "col", None),
            P("grp", "row", None),
            P("grp", None),
            P("grp", None),
            P("grp", None),
        ),
        check_vma=False,
    )
```

```python
import jax
import jax.numpy as jnp
from jax import lax
from jax.experimental import pallas as pl
from jax.experimental.pallas import tpu as pltpu
from jax.sharding import PartitionSpec as P

BF = jnp.bfloat16
F32 = jnp.float32
NN = (((1,), (0,)), ((), ()))
NT = (((1,), (1,)), ((), ()))
TN = (((0,), (0,)), ((), ()))
VMEM = 64 * 1024 * 1024
COST = {'grad_outer_right': 4, 'grad_left_side': 4, 'cut': 20, 'finish_a': 0.5, 'finish_b': 0.2, 'join_send': 2, 'project': 1}
IBLK = 8


def params(vmem=VMEM):
    return pltpu.CompilerParams(vmem_limit_bytes=vmem)


def dot(a, b, dims=NN):
    return lax.dot_general(a, b, dims, preferred_element_type=F32)


def whole(shape):
    return pl.BlockSpec(shape, lambda *_: (0,) * len(shape))


def shape(dims, dtype=BF):
    return jax.ShapeDtypeStruct(dims, dtype)


def far(*values):
    return tuple(pltpu.with_memory_space_constraint(v, pltpu.HBM) for v in values)


def near(*values):
    return tuple(pltpu.with_memory_space_constraint(v, pltpu.VMEM) for v in values)


def sent(dims, dtype=BF):
    return pltpu.HBM(dims, dtype)


def kept(dims, dtype=BF):
    return pltpu.VMEM(dims, dtype)


def call(
    kernel, name, grid, ins, outs, scratch, scalars, arrays, flops, bytes_accessed, vmem=VMEM
):
    return pl.pallas_call(
        kernel,
        name=name,
        grid_spec=pltpu.PrefetchScalarGridSpec(
            num_scalar_prefetch=len(scalars),
            grid=grid,
            in_specs=ins,
            out_specs=[o[0] for o in outs],
            scratch_shapes=scratch,
        ),
        out_shape=[o[1] for o in outs],
        compiler_params=params(vmem),
        cost_estimate=pl.CostEstimate(
            flops=int(COST.get(name, 0) * 1e9), bytes_accessed=1024, transcendentals=0
        ),
    )(*scalars, *arrays)


def depth_rows(cov, lanes):
    total = jnp.sum(cov.astype(F32), axis=1, keepdims=True)
    return jnp.broadcast_to(total, (cov.shape[0], lanes))


def depth_lanes(cov):
    row = depth_rows(cov, cov.shape[0]).T[0:1, :]
    return jnp.concatenate([row, row], axis=1)


def project(cov_t, alignment, gain, bias, wr_t):
    seqs, rows, chans = alignment.shape
    narrow = wr_t.shape[0]
    half = seqs // 2
    blk = 16
    steps = half // blk
    wide = rows * narrow

    def kernel(
        cov_ref, x_ref, gain_ref, bias_ref, w_ref, normed_ref, xhat_ref, stat_ref, r_ref, ys, nbs
    ):
        n = pl.program_id(0)
        gain_v = gain_ref[...]
        bias_v = bias_ref[...]
        lane = lax.broadcasted_iota(jnp.int32, (rows, 128), 1)
        for s2 in range(2):
            for g in range(blk):
                if g % 8 == 0:
                    stat = jnp.zeros((rows, 128), F32)
                x = x_ref[s2, g].astype(F32)
                mean = jnp.mean(x, axis=-1, keepdims=True)
                c = x - mean
                inv = lax.rsqrt(jnp.mean(c * c, axis=-1, keepdims=True) + 1e-05)
                xhat = c * inv
                nb = (xhat * gain_v + bias_v).astype(BF)
                normed_ref[s2, g] = nb
                xhat_ref[s2, g] = xhat.astype(BF)
                at = (2 * g + s2) * rows
                nbs[at : at + rows, :] = nb
                stat = jnp.where(lane == g % 8, inv, stat)
                stat_ref[s2, g // 8] = stat
        y = dot(w_ref[...], nbs[...], NT)
        for g in range(blk):
            at = (n * blk + g) * narrow
            ys[pl.ds(pl.multiple_of(at, narrow), narrow), :] = y[
                :, g * 2 * rows : (g + 1) * 2 * rows
            ]

        @pl.when(n == steps - 1)
        def _():
            lanes = lax.broadcasted_iota(jnp.int32, (half, 2 * rows), 1)
            seq = lax.broadcasted_iota(jnp.int32, (half, 2 * rows), 0).astype(F32)
            low = lanes < rows
            dep = depth_lanes(cov_ref[...])
            top_on = seq < dep
            bot_on = seq + half < dep
            for dp in range(narrow // 2):
                even = ys[pl.ds(2 * dp, half, stride=narrow), :]
                odd = ys[pl.ds(2 * dp + 1, half, stride=narrow), :]
                top = jnp.where(low, even, pltpu.roll(odd, rows, 1))
                bot = jnp.where(low, pltpu.roll(even, rows, 1), odd)
                at = slice(dp * 2 * rows, (dp + 1) * 2 * rows)
                r_ref[0:half, at] = jnp.where(top_on, top, 0.0).astype(BF)
                r_ref[half : 2 * half, at] = jnp.where(bot_on, bot, 0.0).astype(BF)

    tile = pl.BlockSpec((2, blk, rows, chans), lambda n: (0, n, 0, 0))
    return call(
        kernel,
        "project",
        (steps,),
        [
            whole(cov_t.shape),
            tile,
            whole((1, chans)),
            whole((1, chans)),
            whole(wr_t.shape),
        ],
        [
            (tile, shape((2, half, rows, chans))),
            (tile, shape((2, half, rows, chans))),
            (
                pl.BlockSpec((2, blk // 8, rows, 128), lambda n: (0, n, 0, 0)),
                shape((2, half // 8, rows, 128), F32),
            ),
            (whole((seqs, wide)), shape((seqs, wide))),
        ],
        [
            pltpu.VMEM((half * narrow, 2 * rows), F32),
            pltpu.VMEM((2 * blk * rows, chans), BF),
        ],
        (),
        (
            cov_t,
            alignment.reshape(2, half, rows, chans),
            gain[None, :],
            bias[None, :],
            wr_t,
        ),
        2e9,
        7e6,
    )


def pair_block(a, b):
    z = jnp.zeros_like(a)
    return jnp.concatenate(
        [
            jnp.concatenate([a, z], axis=1),
            jnp.concatenate([z, a], axis=1),
            jnp.concatenate([b, z], axis=1),
            jnp.concatenate([z, b], axis=1),
        ],
        axis=0,
    )


def rows_at(p, count):
    start = p * count
    if count % 8 == 0:
        start = pl.multiple_of(start, 8)
    return pl.ds(start, count)


def send_pieces(me, acc, outs):
    rows = outs[0].shape[0]
    count = len(outs)
    for t, out in enumerate(outs):
        p = lax.rem(me + t, count)
        out[...] = acc[rows_at(p, rows), :].astype(out.dtype)


def right_side(own, me, cov_t, cov_far, cot, out_weight, wl_t, normed, block, pieces, piece_rows):
    rows, _, pair = cot.shape
    seqs, _, chans = normed.shape
    cols = cov_far.shape[0]
    narrow = wl_t.shape[0]
    wide = rows * narrow
    c_wide = cols * narrow
    i_blk = 16

    def kernel(
        own_ref,
        me_ref,
        cov_ref,
        far_ref,
        cot_ref,
        wo_ref,
        wl_ref,
        n_ref,
        s_ref,
        g_ref,
        w2_ref,
        lt_ref,
        dcol,
        *rest,
    ):
        outs = rest[:pieces]
        acc, wide_f, z, drow = rest[pieces:]
        n = pl.program_id(0)

        @pl.when(n == 0)
        def _():
            acc[...] = jnp.zeros_like(acc)
            drow[...] = depth_rows(cov_ref[...], 128)
            mine = (own_ref[0] == 1).astype(F32)
            far = depth_rows(far_ref[...], 128)
            dcol[...] = mine * drow[...] + (1.0 - mine) * far
            wide_f[...] = wo_ref[...].astype(F32)
            for dp in range(narrow // 2):
                for d2 in range(2):
                    v = wide_f[pl.ds(2 * dp + d2, narrow, stride=narrow), :]
                    w2_ref[dp * narrow : (dp + 1) * narrow, d2 * pair : (d2 + 1) * pair] = (
                        v.astype(BF)
                    )

        dep = dcol[...]
        w = w2_ref[...]
        mine_rows = drow[pl.ds(pl.multiple_of(n * i_blk, i_blk), i_blk), :]
        blk = n_ref[...].astype(F32).reshape(seqs * i_blk, chans).astype(BF)
        z[...] = dot(blk, wl_ref[...], NT)
        seq = lax.broadcasted_iota(jnp.int32, (seqs, narrow), 0).astype(F32)
        per = 128 // narrow
        tiles = []
        for q in range(i_blk // per):
            parts = []
            for k in range(per):
                i = q * per + k
                v = z[pl.ds(i, seqs, stride=i_blk), :]
                parts.append(jnp.where(seq < mine_rows[i : i + 1, :narrow], v, 0.0))
            tile = jnp.concatenate(parts, axis=1)
            lt_ref[q * 128 : (q + 1) * 128, :] = tile.T.astype(BF)
            tiles.append(tile.astype(BF))
        left = jnp.concatenate(tiles, axis=1)
        for ip in range(i_blk // 2):
            scaled = []
            for k in range(2):
                i = 2 * ip + k
                den = jnp.maximum(jnp.minimum(dep, mine_rows[i : i + 1, :]), 1.0)
                s = (cot_ref[i].astype(F32) / den).astype(BF)
                s_ref[i] = s
                scaled.append(s)
            g = dot(w, pair_block(*scaled), NT).astype(BF)
            for k in range(2):
                i = 2 * ip + k
                for dp in range(narrow // 2):
                    g_ref[
                        i * narrow : (i + 1) * narrow, dp * 2 * cols : (dp + 1) * 2 * cols
                    ] = g[dp * narrow : (dp + 1) * narrow, k * 2 * cols : (k + 1) * 2 * cols]
        acc[0:seqs, :] += dot(left, g_ref[...])

        @pl.when(n == pl.num_programs(0) - 1)
        def _():
            send_pieces(me_ref[0], acc, outs)

    return call(
        kernel,
        "grad_outer_right",
        (rows // i_blk,),
        [
            whole(cov_t.shape),
            whole(cov_far.shape),
            pl.BlockSpec((i_blk, cols, pair), lambda n, *_: (n, block, 0)),
            whole(out_weight.shape),
            whole(wl_t.shape),
            pl.BlockSpec((seqs, i_blk, chans), lambda n, *_: (0, n, 0)),
        ],
        [
            (
                pl.BlockSpec((i_blk, cols, pair), lambda n, *_: (n, 0, 0)),
                kept((rows, cols, pair)),
            ),
            (pl.BlockSpec((i_blk * narrow, c_wide), lambda n, *_: (n, 0)), kept((wide, c_wide))),
            (
                whole((narrow * narrow // 2, 2 * pair)),
                kept((narrow * narrow // 2, 2 * pair)),
            ),
            (pl.BlockSpec((i_blk * narrow, seqs), lambda n, *_: (n, 0)), kept((wide, seqs))),
            (whole((cols, 128)), kept((cols, 128), F32)),
        ]
        + [(whole((piece_rows, c_wide)), sent((piece_rows, c_wide)))] * pieces,
        [
            pltpu.VMEM((piece_rows * pieces, c_wide), F32),
            pltpu.VMEM(out_weight.shape, F32),
            pltpu.VMEM((seqs * i_blk, narrow), F32),
            pltpu.VMEM((rows, 128), F32),
        ],
        (own, me),
        far(cov_t, cov_far, cot, out_weight, wl_t, normed),
        4e9,
        16e6,
        VMEM // 2,
    )


def forward(me, cov_t, left_t, right, scaled, w2, dcol, bias, pieces):
    rows, cols, pair = scaled.shape
    wide, seqs = left_t.shape
    narrow = wide // rows
    c_wide = cols * narrow
    i_blk = IBLK
    high = narrow * narrow // 2
    part = high // pieces

    def kernel(
        me_ref, cov_ref, lt_ref, r_ref, s_ref, w2_ref, dcol_ref, bias_ref, pu_ref, *rest
    ):
        outs = rest[:-3]
        acc, w2t, drow = rest[-3:]
        n = pl.program_id(0)

        @pl.when(n == 0)
        def _():
            acc[...] = jnp.zeros_like(acc)
            w2t[...] = w2_ref[...].astype(F32).T.astype(BF)
            drow[...] = depth_rows(cov_ref[...], 128)

        lane = lax.broadcasted_iota(jnp.int32, (pair, 2 * cols), 1)
        low = lane < cols
        dep = dcol_ref[...]
        mine_rows = drow[pl.ds(pl.multiple_of(n * i_blk, i_blk), i_blk), :]
        outer = dot(lt_ref[...], r_ref[...]).astype(BF)
        x = jnp.concatenate(
            [
                jnp.concatenate(
                    [
                        outer[
                            i * narrow : (i + 1) * narrow, dp * 2 * cols : (dp + 1) * 2 * cols
                        ]
                        for dp in range(narrow // 2)
                    ],
                    axis=0,
                )
                for i in range(i_blk)
            ],
            axis=1,
        )
        sbd = jnp.concatenate(
            [pair_block(s_ref[2 * k], s_ref[2 * k + 1]) for k in range(i_blk // 2)], axis=0
        )
        acc[...] += dot(x, sbd)
        pt = dot(w2t[...], x)
        for ip in range(i_blk // 2):
            at = ip * 4 * cols
            e0, o0 = pt[:pair, at : at + 2 * cols], pt[:pair, at + 2 * cols : at + 4 * cols]
            e1, o1 = pt[pair:, at : at + 2 * cols], pt[pair:, at + 2 * cols : at + 4 * cols]
            both = jnp.where(low, e0, o1) + pltpu.roll(jnp.where(low, o0, e1), cols, 1)
            both = both.T + bias_ref[...]
            for k in range(2):
                i = 2 * ip + k
                den = jnp.maximum(jnp.minimum(dep, mine_rows[i : i + 1, :]), 1.0)
                pu_ref[i] = (both[k * cols : (k + 1) * cols] / den).astype(BF)

        @pl.when(n == pl.num_programs(0) - 1)
        def _():
            send_pieces(me_ref[0], acc, outs)

    return call(
        kernel,
        "forward",
        (rows // i_blk,),
        [
            whole(cov_t.shape),
            pl.BlockSpec((i_blk * narrow, seqs), lambda n, *_: (n, 0)),
            whole(right.shape),
            pl.BlockSpec((i_blk, cols, pair), lambda n, *_: (n, 0, 0)),
            whole(w2.shape),
            whole(dcol.shape),
            whole((1, pair)),
        ],
        [
            (
                pl.BlockSpec((i_blk, cols, pair), lambda n, *_: (n, 0, 0)),
                sent((rows, cols, pair)),
            ),
            (whole((part, 2 * pair)), sent((part, 2 * pair), F32)),
        ]
        + [(whole((part, 2 * pair)), sent((part, 2 * pair)))] * (pieces - 1),
        [
            pltpu.VMEM((high, 2 * pair), F32),
            pltpu.VMEM((w2.shape[1], w2.shape[0]), BF),
            pltpu.VMEM((rows, 128), F32),
        ],
        (me,),
        (*far(cov_t), *near(left_t, right, scaled, w2, dcol), *far(bias[None, :])),
        6e9,
        6e6,
        VMEM // 2,
    )


def left_side(sel, me, grad_outer, rights, pieces, piece_rows):
    wide, c_wide = grad_outer.shape
    seqs = rights[0].shape[0]
    chunk = 512

    def kernel(sel_ref, me_ref, g_ref, *rest):
        r_in = rest[: len(rights)]
        r_ref, outs, acc = rest[len(rights)], rest[len(rights) + 1 : -1], rest[-1]
        n = pl.program_id(0)

        @pl.when(n == 0)
        def _():
            acc[...] = jnp.zeros_like(acc)
            for t, r in enumerate(r_in):

                @pl.when(sel_ref[0] == t)
                def _():
                    pltpu.sync_copy(r, r_ref)

        at = pl.ds(pl.multiple_of(n * chunk, chunk), chunk)
        acc[0:seqs, at] = dot(g_ref[...], r_ref[...], NT).T

        @pl.when(n == pl.num_programs(0) - 1)
        def _():
            send_pieces(me_ref[0], acc, outs)

    return call(
        kernel,
        "grad_left_side",
        (wide // chunk,),
        [pl.BlockSpec((chunk, c_wide), lambda n, *_: (n, 0))]
        + [pl.BlockSpec(memory_space=pl.ANY)] * len(rights),
        [(whole((seqs, c_wide)), kept((seqs, c_wide)))]
        + [(whole((piece_rows, wide)), sent((piece_rows, wide)))] * pieces,
        [pltpu.VMEM((piece_rows * pieces, wide), F32)],
        (sel, me),
        (*near(grad_outer), *rights),
        2e9,
        9e6,
        VMEM // 2,
    )


def tokens(me, cov_t, stat, lefts, rights, normed):
    seqs, rows, chans = normed.shape
    piece_rows, wide = lefts[0].shape
    narrow = wide // rows
    count = piece_rows * rows
    h = count // 2
    quad = 4 * rows
    last = seqs // piece_rows - 1
    per_half = (last + 1) // 2
    n_l, n_r = len(lefts), len(rights)
    nar2 = 2 * narrow

    def kernel(me_ref, cov_ref, stat_ref, n_ref, *rest):
        l_in = rest[:n_l]
        r_in = rest[n_l : n_l + n_r]
        out, z, t = rest[n_l + n_r :]
        plain = []
        base = (me_ref[0] * piece_rows).astype(F32)
        left = sum(ref[...].astype(F32) for ref in l_in)
        right = sum(ref[...].astype(F32) for ref in r_in)
        drow = depth_rows(cov_ref[...], 128)
        seq = lax.broadcasted_iota(jnp.int32, (piece_rows, narrow), 0).astype(F32) + base
        seq2 = lax.broadcasted_iota(jnp.int32, (piece_rows, 2 * rows), 0).astype(F32) + base
        on = seq2 < depth_lanes(cov_ref[...])
        for i in range(rows):
            v = jnp.where(
                seq < drow[i : i + 1, :narrow], left[:, i * narrow : (i + 1) * narrow], 0.0
            )
            z[pl.ds(i, piece_rows, stride=rows), 0:narrow] = v
        for dp in range(narrow // 2):
            v = jnp.where(on, right[:, dp * 2 * rows : (dp + 1) * 2 * rows], 0.0)
            t[pl.ds(2 * dp, piece_rows, stride=narrow), :] = v[:, :rows]
            t[pl.ds(2 * dp + 1, piece_rows, stride=narrow), :] = v[:, rows:]
        per = 128 // narrow
        for q in range(piece_rows // per):
            tr = t[q * 128 : (q + 1) * 128, :].T
            for k in range(per):
                s = q * per + k
                z[s * rows : (s + 1) * rows, narrow:nar2] = tr[:, k * narrow : (k + 1) * narrow]
        for b in range(piece_rows // 8):
            at = b * 2 * quad
            stats = stat_ref[0, b]
            pair_up, scaled = [], []
            for half in range(2):
                v = z[at + half * quad : at + (half + 1) * quad, :]
                inv = [
                    jnp.broadcast_to(stats[:, 4 * half + j : 4 * half + j + 1], (rows, nar2))
                    for j in range(4)
                ]
                pair_up.append(v)
                scaled.append(v * jnp.concatenate(inv, axis=0))
            out[b * quad : (b + 1) * quad, :] = jnp.concatenate(scaled, axis=1).astype(BF)
            plain.append(jnp.concatenate(pair_up, axis=1).astype(BF))
        v = jnp.concatenate(plain, axis=0)
        nb = n_ref[...].reshape(piece_rows // 8, 2, quad, chans)
        top = dot(v, nb[:, 0].reshape(h, chans), TN)
        bot = dot(v, nb[:, 1].reshape(h, chans), TN)
        grads = (top[:nar2] + bot[nar2:]).astype(BF)
        for k in range(chans // 128):
            out[h + k * nar2 : h + (k + 1) * nar2, :] = grads[:, k * 128 : (k + 1) * 128]

    return call(
        kernel,
        "tokens",
        (1,),
        [
            whole(cov_t.shape),
            pl.BlockSpec(
                (1, piece_rows // 8, rows, 128),
                lambda n, me: (
                    jnp.minimum(me[0], last) // per_half,
                    jnp.minimum(me[0], last) % per_half,
                    0,
                    0,
                ),
            ),
            pl.BlockSpec(
                (piece_rows, rows, chans), lambda n, me: (jnp.minimum(me[0], last), 0, 0)
            ),
        ]
        + [whole((piece_rows, wide))] * (n_l + n_r),
        [(whole((h + nar2 * chans // 128, 128)), shape((h + nar2 * chans // 128, 128)))],
        [pltpu.VMEM((count, nar2), F32), pltpu.VMEM((piece_rows * narrow, rows), F32)],
        (me,),
        (cov_t, stat, normed, *lefts, *rights),
        4e8,
        2e6,
    )[0]


def cut(me, parts, pieces):
    m, lanes = parts[0].shape

    def kernel(me_ref, *rest):
        ins, outs, acc = rest[: len(parts)], rest[len(parts) : -1], rest[-1]
        acc[...] = sum(ref[...].astype(F32) for ref in ins)
        send_pieces(me_ref[0], acc, outs)

    return call(
        kernel,
        "cut",
        (1,),
        [whole((m, lanes))] * len(parts),
        [(whole((m // pieces, lanes)), shape((m // pieces, lanes), F32))] * pieces,
        [pltpu.VMEM((m, lanes), F32)],
        (me,),
        tuple(parts),
        1e6,
        1e6,
    )


def finish(me, qs, alignment, wl_t, wr_t, gain, first, count, before=None):
    seqs, rows, chans = alignment.shape
    pieces = len(qs)
    quad = 4 * rows
    nar2 = 2 * wl_t.shape[0]
    blocks = (qs[0].shape[0] - nar2 * chans // 128) // quad
    every = count == seqs // (8 * blocks)
    given = () if before is None else (before,)

    def piece(n, me_ref):
        return n if every else me_ref[0] ^ (n + first)

    def kernel(me_ref, x_ref, wl_ref, wr_ref, gain_ref, *rest):
        q_in, (out, wc, q_now) = rest[:pieces], rest[-3:]
        n = pl.program_id(0)

        @pl.when(n == 0)
        def _():
            w = jnp.concatenate([wl_ref[...], wr_ref[...]], axis=0).astype(F32) * gain_ref[...]
            w = w - jnp.mean(w, axis=1, keepdims=True)
            hi = w.astype(BF)
            lo = (w - hi.astype(F32)).astype(BF)
            none = jnp.zeros_like(hi)
            wc[0] = jnp.concatenate([hi, none, lo, none], axis=0)
            wc[1] = jnp.concatenate([none, hi, none, lo], axis=0)

        t = piece(n, me_ref) ^ me_ref[0]
        for k in range(pieces):

            @pl.when(t == k)
            def _():
                q_now[...] = q_in[k][0 : blocks * quad, :]

        for b in range(blocks):
            q = q_now[b * quad : (b + 1) * quad, :]
            both = jnp.concatenate([q, q], axis=1)
            for half in range(2):
                g = dot(both, wc[half])
                for j in range(4):
                    s = half * 4 + j
                    xh = x_ref[8 * b + s].astype(F32)
                    gc = g[j * rows : (j + 1) * rows]
                    m = jnp.mean(gc * xh, axis=-1, keepdims=True)
                    out[8 * b + s] = (gc - xh * m).astype(BF)

    blk = pl.BlockSpec((8 * blocks, rows, chans), lambda n, me_ref: (piece(n, me_ref), 0, 0))
    return pl.pallas_call(
        kernel,
        name="finish",
        grid_spec=pltpu.PrefetchScalarGridSpec(
            num_scalar_prefetch=1,
            grid=(count,),
            in_specs=[
                blk,
                whole(wl_t.shape),
                whole(wr_t.shape),
                whole((1, chans)),
            ]
            + [whole(qs[0].shape)] * pieces
            + [pl.BlockSpec(memory_space=pl.ANY)] * len(given),
            out_specs=blk,
            scratch_shapes=[
                pltpu.VMEM((2, 4 * nar2, chans), BF),
                pltpu.VMEM((blocks * quad, 128), BF),
            ],
        ),
        out_shape=shape(alignment.shape),
        input_output_aliases={5 + pieces: 0} if given else {},
        compiler_params=params(),
        cost_estimate=pl.CostEstimate(
            flops=int(COST.get("finish_a" if before is None else "finish_b", 0) * 1e9),
            bytes_accessed=1024,
            transcendentals=0,
        ),
    )(me, alignment, wl_t, wr_t, gain[None, :], *qs, *given)


def join_send(me, parts, qs, nar2):
    m, lanes = parts[0].shape
    n = len(parts)
    extra = nar2 * lanes // 128
    h = qs[0].shape[0] - extra

    def kernel(me_ref, *rest):
        ins, q_in, out, acc = rest[:n], rest[n:-2], rest[-2], rest[-1]
        for t in range(n):
            p = lax.rem(me_ref[0] - t + n, n)
            acc[rows_at(p, m), :] = ins[t][...]
        total = sum(q[...].astype(F32) for q in q_in)
        g = jnp.concatenate(
            [total[k * nar2 : (k + 1) * nar2] for k in range(lanes // 128)], axis=1
        )
        out[0 : n * m, :] = acc[...].astype(BF)
        out[n * m :, :] = g.astype(BF)

    total = n * m + nar2
    return call(
        kernel,
        "join_send",
        (1,),
        [whole((m, lanes))] * n
        + [pl.BlockSpec((extra, 128), lambda *_: (h // extra, 0))] * len(qs),
        [(whole((total, lanes)), shape((total, lanes)))],
        [pltpu.VMEM((n * m, lanes), F32)],
        (me,),
        (*parts, *qs),
        1e6,
        1e6,
    )[0]


def join_out(me, parts, nar2, narrow):
    rows, lanes = parts[0].shape
    n = len(parts)
    m = rows - nar2
    pair = lanes // 2
    dps = m // narrow

    def kernel(me_ref, *rest):
        ins, (out, lg, rg) = rest[:n], rest[n:]
        for t in range(n):
            p = lax.rem(me_ref[0] - t + n, n)
            v = ins[t][0:m, :].astype(F32)
            for k in range(dps):
                for d2 in range(2):
                    out[pl.ds(2 * (p * dps + k) + d2, narrow, stride=narrow), :] = v[
                        k * narrow : (k + 1) * narrow, d2 * pair : (d2 + 1) * pair
                    ]
        grads = sum(ref[m:, :].astype(F32) for ref in ins)
        lg[...] = grads[:narrow]
        rg[...] = grads[narrow:]

    return call(
        kernel,
        "join_out",
        (1,),
        [whole((rows, lanes))] * n,
        [
            (whole((n * m * 2, pair)), shape((n * m * 2, pair), F32)),
            (whole((narrow, lanes)), shape((narrow, lanes), F32)),
            (whole((narrow, lanes)), shape((narrow, lanes), F32)),
        ],
        [],
        (me,),
        parts,
        1e6,
        1e6,
    )


BOTH = ("row", "col")


def shift(value, axis, t):
    n = lax.axis_size(axis)
    return lax.ppermute(value, axis, [(k, (k + t) % n) for k in range(n)])


def shifts(own, others, axis):
    return [own] + [shift(v, axis, t + 1) for t, v in enumerate(others)]


def swap(value, axis, t):
    n = lax.axis_size(axis)
    return lax.ppermute(value, axis, [(k, k ^ t) for k in range(n)])


def gather(value, axis):
    n = lax.axis_size(axis)
    if n == 4:
        near, far = swap(value, axis, 1), swap(value, axis, 2)
        return [value, near, far, swap(far, axis, 1)]
    return [value] + [swap(value, axis, t) for t in range(1, n)]


def spread_small(value, m, ratio):
    n_row, n_col = lax.axis_size("row"), lax.axis_size("col")
    total = None
    for first in range(1, n_row, n_col - 1):
        pairs = []
        for c in range(n_col):
            b = c * ratio + m
            for k, t in enumerate(range(first, min(first + n_col - 1, n_row))):
                pairs.append((b * n_col + (c + 1 + k) % n_col, (b + t) % n_row * n_col + c))
        got = lax.ppermute(value, BOTH, pairs)
        total = got if total is None else total + got
    return total


def spread(value, m, ratio):
    n_row, n_col = lax.axis_size("row"), lax.axis_size("col")
    out = [value]
    if n_row == 4 and n_col == 4:
        first = [(c * n_col + c, (c ^ 2) * n_col + c) for c in range(n_col)]
        first += [(c * n_col + (c ^ 1), (c ^ 1) * n_col + c) for c in range(n_col)]
        second = [(c * n_col + c, (c ^ 3) * n_col + c) for c in range(n_col)]
        return [value, lax.ppermute(value, BOTH, first), lax.ppermute(value, BOTH, second)]
    for t in range(1, n_row):
        pairs = [
            ((c * ratio + m) * n_col + c, (c * ratio + m + t) % n_row * n_col + c)
            for c in range(n_col)
        ]
        out.append(lax.ppermute(value, BOTH, pairs))
    return out


def spread_choice(row, col, m, ratio):
    n_row, n_col = lax.axis_size("row"), lax.axis_size("col")
    if n_row == 4 and n_col == 4:
        apart = row ^ col
        return jnp.where(apart == 3, 2, jnp.where(apart == 0, 0, 1))
    return (row - (col * ratio + m) + n_row) % n_row


def to_owners(pieces, ratio):
    n_row, n_col = lax.axis_size("row"), lax.axis_size("col")
    row = lax.axis_index("row")
    if ratio > 1:
        stacked = jnp.stack(pieces)
        pieces = [
            lax.dynamic_index_in_dim(stacked, (row + t) % n_row, 0, keepdims=False)
            for t in range(n_row)
        ]
    parts = []
    for t, piece in enumerate(pieces):
        pairs = []
        for r in range(n_row):
            m, k = divmod((r + t) % n_row, n_col)
            pairs += [(r * n_col + c, (c * ratio + m) * n_col + k) for c in range(n_col)]
        parts.append(lax.ppermute(piece, BOTH, pairs))
    return parts


def one(value):
    return value[None].astype(jnp.int32)


def body(
    alignment,
    coverage,
    layer_norm_gain,
    layer_norm_bias,
    left_weight,
    right_weight,
    out_weight,
    out_bias,
    cotangent,
):
    n_row, n_col = lax.axis_size("row"), lax.axis_size("col")
    ratio = n_row // n_col
    row_index = lax.axis_index("row")
    col_index = lax.axis_index("col")
    me_row, me_col = one(row_index), one(col_index)
    seqs, rows, chans = alignment.shape
    narrow = left_weight.shape[1]
    pair = out_weight.shape[1]
    piece_rows = (seqs // n_col + 7) // 8 * 8
    cov_t = coverage.T
    wl_t, wr_t = left_weight.T, right_weight.T

    cov_far = [spread_small(cov_t, m, ratio) for m in range(ratio)]
    normed, xhat, stat, right = project(cov_t, alignment, layer_norm_gain, layer_norm_bias, wr_t)
    right, cov_far = lax.optimization_barrier((right, cov_far))
    normed = normed.reshape(seqs, rows, chans)
    xhat = xhat.reshape(seqs, rows, chans)

    right_pieces, firsts = [], []
    for m in range(ratio):
        own = one(row_index == col_index * ratio + m)
        turn_by = one(row_index) if ratio == 1 else jnp.zeros_like(me_row)
        scaled, grad_outer, w2, left_t, dcol, *pieces = right_side(
            own,
            turn_by,
            cov_t,
            cov_far[m],
            cotangent,
            out_weight,
            wl_t,
            normed,
            m,
            n_col,
            piece_rows,
        )
        firsts.append((scaled, grad_outer, w2, left_t, dcol))
        right_pieces.extend(pieces)
    right_parts = to_owners(right_pieces, ratio)

    left_pieces, updates, weight_pieces = None, [], None
    for m in range(ratio):
        scaled, grad_outer, w2, left_t, dcol = firsts[m]
        sel = one(spread_choice(row_index, col_index, m, ratio))
        right_cols, *pieces = left_side(
            sel, me_col, grad_outer, spread(right, m, ratio), n_col, piece_rows
        )
        update, *gw = forward(
            me_row, cov_t, left_t, right_cols, scaled, w2, dcol, out_bias, n_row
        )
        updates.append(update)
        if m == 0:
            left_pieces, weight_pieces = pieces, gw
        else:
            left_pieces = [(a.astype(F32) + b).astype(BF) for a, b in zip(left_pieces, pieces)]
            weight_pieces = [
                (a.astype(F32) + b).astype(a.dtype) for a, b in zip(weight_pieces, gw)
            ]
    pair_update = updates[0] if ratio == 1 else jnp.concatenate(updates, axis=1)

    gw_parts = shifts(weight_pieces[0], weight_pieces[1:], "row")
    lefts = shifts(left_pieces[0], left_pieces[1:], "col")
    lefts, pair_update = lax.optimization_barrier((lefts, pair_update))
    q = tokens(me_col, cov_t, stat, lefts, right_parts, normed)
    qs = gather(q, "col")

    if weight_pieces[0].shape[0] % (8 * n_col) == 0:
        pieces = cut(me_col, gw_parts, n_col)
        part = sum(shifts(pieces[0], pieces[1:], "col"))
        parts = [part] + [shift(part, "col", t) for t in range(1, n_col)]
    else:
        parts = [lax.psum(cut(me_col, gw_parts, 1)[0], "col")]
    ends = (xhat, wl_t, wr_t, layer_norm_gain)
    if n_col == 4:
        gradient = finish(me_col, [qs[0], qs[1]], *ends, 0, 2)
        gradient, parts = lax.optimization_barrier((gradient, parts))
    last = join_send(me_col, parts, qs, 2 * narrow)
    lasts = [last] + [shift(last, "row", t) for t in range(1, n_row)]
    if n_col == 4:
        gradient = finish(me_col, qs, *ends, 2, 2, gradient)
    else:
        gradient = finish(me_col, qs, *ends, 0, seqs // piece_rows)
    lasts, gradient = lax.optimization_barrier((lasts, gradient))
    grad_out, grad_left, grad_right = join_out(me_row, lasts, 2 * narrow, narrow)
    return pair_update, gradient, grad_left.T, grad_right.T, grad_out


def solution(mesh):
    return jax.shard_map(
        body,
        mesh=mesh,
        in_specs=(
            P("grp", "row", None),
            P("grp", "row"),
            P(),
            P(),
            P(),
            P(),
            P(),
            P(),
            P(("grp", "row"), "col", None),
        ),
        out_specs=(
            P(("grp", "row"), "col", None),
            P("grp", "row", None),
            P("grp", None),
            P("grp", None),
            P("grp", None),
        ),
        check_vma=False,
    )
```

```python
import jax
import jax.numpy as jnp
from jax import lax
from jax.experimental import pallas as pl
from jax.experimental.pallas import tpu as pltpu
from jax.sharding import PartitionSpec as P

BF = jnp.bfloat16
F32 = jnp.float32
NN = (((1,), (0,)), ((), ()))
NT = (((1,), (1,)), ((), ()))
TN = (((0,), (0,)), ((), ()))
VMEM = 64 * 1024 * 1024
COST = {'grad_outer_right': 4, 'grad_left_side': 4, 'cut': 20, 'finish_a': 2, 'finish_b': 6, 'join_send': 2, 'project': 1}
IBLK = 8


def params(vmem=VMEM):
    return pltpu.CompilerParams(vmem_limit_bytes=vmem)


def dot(a, b, dims=NN):
    return lax.dot_general(a, b, dims, preferred_element_type=F32)


def whole(shape):
    return pl.BlockSpec(shape, lambda *_: (0,) * len(shape))


def shape(dims, dtype=BF):
    return jax.ShapeDtypeStruct(dims, dtype)


def far(*values):
    return tuple(pltpu.with_memory_space_constraint(v, pltpu.HBM) for v in values)


def near(*values):
    return tuple(pltpu.with_memory_space_constraint(v, pltpu.VMEM) for v in values)


def sent(dims, dtype=BF):
    return pltpu.HBM(dims, dtype)


def kept(dims, dtype=BF):
    return pltpu.VMEM(dims, dtype)


def call(
    kernel, name, grid, ins, outs, scratch, scalars, arrays, flops, bytes_accessed, vmem=VMEM
):
    return pl.pallas_call(
        kernel,
        name=name,
        grid_spec=pltpu.PrefetchScalarGridSpec(
            num_scalar_prefetch=len(scalars),
            grid=grid,
            in_specs=ins,
            out_specs=[o[0] for o in outs],
            scratch_shapes=scratch,
        ),
        out_shape=[o[1] for o in outs],
        compiler_params=params(vmem),
        cost_estimate=pl.CostEstimate(
            flops=int(COST.get(name, 0) * 1e9), bytes_accessed=1024, transcendentals=0
        ),
    )(*scalars, *arrays)


def depth_rows(cov, lanes):
    total = jnp.sum(cov.astype(F32), axis=1, keepdims=True)
    return jnp.broadcast_to(total, (cov.shape[0], lanes))


def depth_lanes(cov):
    row = depth_rows(cov, cov.shape[0]).T[0:1, :]
    return jnp.concatenate([row, row], axis=1)


def project(cov_t, alignment, gain, bias, wr_t):
    seqs, rows, chans = alignment.shape
    narrow = wr_t.shape[0]
    half = seqs // 2
    blk = 16
    steps = half // blk
    wide = rows * narrow

    def kernel(
        cov_ref, x_ref, gain_ref, bias_ref, w_ref, normed_ref, xhat_ref, stat_ref, r_ref, ys, nbs
    ):
        n = pl.program_id(0)
        gain_v = gain_ref[...]
        bias_v = bias_ref[...]
        lane = lax.broadcasted_iota(jnp.int32, (rows, 128), 1)
        for s2 in range(2):
            for g in range(blk):
                if g % 8 == 0:
                    stat = jnp.zeros((rows, 128), F32)
                x = x_ref[s2, g].astype(F32)
                mean = jnp.mean(x, axis=-1, keepdims=True)
                c = x - mean
                inv = lax.rsqrt(jnp.mean(c * c, axis=-1, keepdims=True) + 1e-05)
                xhat = c * inv
                nb = (xhat * gain_v + bias_v).astype(BF)
                normed_ref[s2, g] = nb
                xhat_ref[s2, g] = xhat.astype(BF)
                at = (2 * g + s2) * rows
                nbs[at : at + rows, :] = nb
                stat = jnp.where(lane == g % 8, inv, stat)
                stat_ref[s2, g // 8] = stat
        y = dot(w_ref[...], nbs[...], NT)
        for g in range(blk):
            at = (n * blk + g) * narrow
            ys[pl.ds(pl.multiple_of(at, narrow), narrow), :] = y[
                :, g * 2 * rows : (g + 1) * 2 * rows
            ]

        @pl.when(n == steps - 1)
        def _():
            lanes = lax.broadcasted_iota(jnp.int32, (half, 2 * rows), 1)
            seq = lax.broadcasted_iota(jnp.int32, (half, 2 * rows), 0).astype(F32)
            low = lanes < rows
            dep = depth_lanes(cov_ref[...])
            top_on = seq < dep
            bot_on = seq + half < dep
            for dp in range(narrow // 2):
                even = ys[pl.ds(2 * dp, half, stride=narrow), :]
                odd = ys[pl.ds(2 * dp + 1, half, stride=narrow), :]
                top = jnp.where(low, even, pltpu.roll(odd, rows, 1))
                bot = jnp.where(low, pltpu.roll(even, rows, 1), odd)
                at = slice(dp * 2 * rows, (dp + 1) * 2 * rows)
                r_ref[0:half, at] = jnp.where(top_on, top, 0.0).astype(BF)
                r_ref[half : 2 * half, at] = jnp.where(bot_on, bot, 0.0).astype(BF)

    tile = pl.BlockSpec((2, blk, rows, chans), lambda n: (0, n, 0, 0))
    return call(
        kernel,
        "project",
        (steps,),
        [
            whole(cov_t.shape),
            tile,
            whole((1, chans)),
            whole((1, chans)),
            whole(wr_t.shape),
        ],
        [
            (tile, sent((2, half, rows, chans))),
            (tile, kept((2, half, rows, chans))),
            (
                pl.BlockSpec((2, blk // 8, rows, 128), lambda n: (0, n, 0, 0)),
                sent((2, half // 8, rows, 128), F32),
            ),
            (whole((seqs, wide)), sent((seqs, wide))),
        ],
        [
            pltpu.VMEM((half * narrow, 2 * rows), F32),
            pltpu.VMEM((2 * blk * rows, chans), BF),
        ],
        (),
        far(
            cov_t,
            alignment.reshape(2, half, rows, chans),
            gain[None, :],
            bias[None, :],
            wr_t,
        ),
        2e9,
        7e6,
        VMEM // 2,
    )


def pair_block(a, b):
    z = jnp.zeros_like(a)
    return jnp.concatenate(
        [
            jnp.concatenate([a, z], axis=1),
            jnp.concatenate([z, a], axis=1),
            jnp.concatenate([b, z], axis=1),
            jnp.concatenate([z, b], axis=1),
        ],
        axis=0,
    )


def rows_at(p, count):
    start = p * count
    if count % 8 == 0:
        start = pl.multiple_of(start, 8)
    return pl.ds(start, count)


def send_pieces(me, acc, outs):
    rows = outs[0].shape[0]
    count = len(outs)
    for t, out in enumerate(outs):
        p = lax.rem(me + t, count)
        out[...] = acc[rows_at(p, rows), :].astype(out.dtype)


def right_side(own, me, cov_t, cov_far, cot, out_weight, wl_t, normed, block, pieces, piece_rows):
    rows, _, pair = cot.shape
    half, chans = normed.shape[1], normed.shape[3]
    seqs = 2 * half
    cols = cov_far.shape[0]
    narrow = wl_t.shape[0]
    wide = rows * narrow
    c_wide = cols * narrow
    i_blk = 16

    def kernel(
        own_ref,
        me_ref,
        cov_ref,
        far_ref,
        cot_ref,
        wo_ref,
        wl_ref,
        n_ref,
        s_ref,
        g_ref,
        w2_ref,
        lt_ref,
        dcol,
        *rest,
    ):
        outs = rest[:pieces]
        acc, wide_f, z, drow = rest[pieces:]
        n = pl.program_id(0)

        @pl.when(n == 0)
        def _():
            acc[...] = jnp.zeros_like(acc)
            drow[...] = depth_rows(cov_ref[...], 128)
            mine = (own_ref[0] == 1).astype(F32)
            far = depth_rows(far_ref[...], 128)
            dcol[...] = mine * drow[...] + (1.0 - mine) * far
            wide_f[...] = wo_ref[...].astype(F32)
            for dp in range(narrow // 2):
                for d2 in range(2):
                    v = wide_f[pl.ds(2 * dp + d2, narrow, stride=narrow), :]
                    w2_ref[dp * narrow : (dp + 1) * narrow, d2 * pair : (d2 + 1) * pair] = (
                        v.astype(BF)
                    )

        dep = dcol[...]
        w = w2_ref[...]
        mine_rows = drow[pl.ds(pl.multiple_of(n * i_blk, i_blk), i_blk), :]
        blk = n_ref[...].astype(F32).reshape(seqs * i_blk, chans).astype(BF)
        z[...] = dot(blk, wl_ref[...], NT)
        seq = lax.broadcasted_iota(jnp.int32, (seqs, narrow), 0).astype(F32)
        per = 128 // narrow
        tiles = []
        for q in range(i_blk // per):
            parts = []
            for k in range(per):
                i = q * per + k
                v = z[pl.ds(i, seqs, stride=i_blk), :]
                parts.append(jnp.where(seq < mine_rows[i : i + 1, :narrow], v, 0.0))
            tile = jnp.concatenate(parts, axis=1)
            lt_ref[q * 128 : (q + 1) * 128, :] = tile.T.astype(BF)
            tiles.append(tile.astype(BF))
        left = jnp.concatenate(tiles, axis=1)
        for ip in range(i_blk // 2):
            scaled = []
            for k in range(2):
                i = 2 * ip + k
                den = jnp.maximum(jnp.minimum(dep, mine_rows[i : i + 1, :]), 1.0)
                s = (cot_ref[i].astype(F32) / den).astype(BF)
                s_ref[i] = s
                scaled.append(s)
            g = dot(w, pair_block(*scaled), NT).astype(BF)
            for k in range(2):
                i = 2 * ip + k
                for dp in range(narrow // 2):
                    g_ref[
                        i * narrow : (i + 1) * narrow, dp * 2 * cols : (dp + 1) * 2 * cols
                    ] = g[dp * narrow : (dp + 1) * narrow, k * 2 * cols : (k + 1) * 2 * cols]
        acc[0:seqs, :] += dot(left, g_ref[...])

        @pl.when(n == pl.num_programs(0) - 1)
        def _():
            send_pieces(me_ref[0], acc, outs)

    return call(
        kernel,
        "grad_outer_right",
        (rows // i_blk,),
        [
            whole(cov_t.shape),
            whole(cov_far.shape),
            pl.BlockSpec((i_blk, cols, pair), lambda n, *_: (n, block, 0)),
            whole(out_weight.shape),
            whole(wl_t.shape),
            pl.BlockSpec((2, half, i_blk, chans), lambda n, *_: (0, 0, n, 0)),
        ],
        [
            (
                pl.BlockSpec((i_blk, cols, pair), lambda n, *_: (n, 0, 0)),
                kept((rows, cols, pair)),
            ),
            (pl.BlockSpec((i_blk * narrow, c_wide), lambda n, *_: (n, 0)), kept((wide, c_wide))),
            (
                whole((narrow * narrow // 2, 2 * pair)),
                kept((narrow * narrow // 2, 2 * pair)),
            ),
            (pl.BlockSpec((i_blk * narrow, seqs), lambda n, *_: (n, 0)), kept((wide, seqs))),
            (whole((cols, 128)), kept((cols, 128), F32)),
        ]
        + [(whole((piece_rows, c_wide)), sent((piece_rows, c_wide)))] * pieces,
        [
            pltpu.VMEM((piece_rows * pieces, c_wide), F32),
            pltpu.VMEM(out_weight.shape, F32),
            pltpu.VMEM((seqs * i_blk, narrow), F32),
            pltpu.VMEM((rows, 128), F32),
        ],
        (own, me),
        (*far(cov_t), *near(cov_far), *far(cot, out_weight, wl_t, normed)),
        4e9,
        16e6,
        VMEM // 2,
    )


def forward(me, cov_t, left_t, right, scaled, w2, dcol, bias, pieces):
    rows, cols, pair = scaled.shape
    wide, seqs = left_t.shape
    narrow = wide // rows
    c_wide = cols * narrow
    i_blk = IBLK
    high = narrow * narrow // 2
    part = high // pieces

    def kernel(
        me_ref, cov_ref, lt_ref, r_ref, s_ref, w2_ref, dcol_ref, bias_ref, pu_ref, *rest
    ):
        outs = rest[:-3]
        acc, w2t, drow = rest[-3:]
        n = pl.program_id(0)

        @pl.when(n == 0)
        def _():
            acc[...] = jnp.zeros_like(acc)
            w2t[...] = w2_ref[...].astype(F32).T.astype(BF)
            drow[...] = depth_rows(cov_ref[...], 128)

        lane = lax.broadcasted_iota(jnp.int32, (pair, 2 * cols), 1)
        low = lane < cols
        dep = dcol_ref[...]
        mine_rows = drow[pl.ds(pl.multiple_of(n * i_blk, i_blk), i_blk), :]
        outer = dot(lt_ref[...], r_ref[...]).astype(BF)
        x = jnp.concatenate(
            [
                jnp.concatenate(
                    [
                        outer[
                            i * narrow : (i + 1) * narrow, dp * 2 * cols : (dp + 1) * 2 * cols
                        ]
                        for dp in range(narrow // 2)
                    ],
                    axis=0,
                )
                for i in range(i_blk)
            ],
            axis=1,
        )
        sbd = jnp.concatenate(
            [pair_block(s_ref[2 * k], s_ref[2 * k + 1]) for k in range(i_blk // 2)], axis=0
        )
        acc[...] += dot(x, sbd)
        pt = dot(w2t[...], x)
        for ip in range(i_blk // 2):
            at = ip * 4 * cols
            e0, o0 = pt[:pair, at : at + 2 * cols], pt[:pair, at + 2 * cols : at + 4 * cols]
            e1, o1 = pt[pair:, at : at + 2 * cols], pt[pair:, at + 2 * cols : at + 4 * cols]
            both = jnp.where(low, e0, o1) + pltpu.roll(jnp.where(low, o0, e1), cols, 1)
            both = both.T + bias_ref[...]
            for k in range(2):
                i = 2 * ip + k
                den = jnp.maximum(jnp.minimum(dep, mine_rows[i : i + 1, :]), 1.0)
                pu_ref[i] = (both[k * cols : (k + 1) * cols] / den).astype(BF)

        @pl.when(n == pl.num_programs(0) - 1)
        def _():
            send_pieces(me_ref[0], acc, outs)

    return call(
        kernel,
        "forward",
        (rows // i_blk,),
        [
            whole(cov_t.shape),
            pl.BlockSpec((i_blk * narrow, seqs), lambda n, *_: (n, 0)),
            whole(right.shape),
            pl.BlockSpec((i_blk, cols, pair), lambda n, *_: (n, 0, 0)),
            whole(w2.shape),
            whole(dcol.shape),
            whole((1, pair)),
        ],
        [
            (
                pl.BlockSpec((i_blk, cols, pair), lambda n, *_: (n, 0, 0)),
                sent((rows, cols, pair)),
            ),
            (whole((part, 2 * pair)), sent((part, 2 * pair), F32)),
        ]
        + [(whole((part, 2 * pair)), sent((part, 2 * pair)))] * (pieces - 1),
        [
            pltpu.VMEM((high, 2 * pair), F32),
            pltpu.VMEM((w2.shape[1], w2.shape[0]), BF),
            pltpu.VMEM((rows, 128), F32),
        ],
        (me,),
        (*far(cov_t), *near(left_t, right, scaled, w2, dcol), *far(bias[None, :])),
        6e9,
        6e6,
        VMEM // 2,
    )


def left_side(sel, me, grad_outer, rights, pieces, piece_rows):
    wide, c_wide = grad_outer.shape
    seqs = rights[0].shape[0]
    chunk = 512

    def kernel(sel_ref, me_ref, g_ref, *rest):
        r_in = rest[: len(rights)]
        r_ref, outs, acc = rest[len(rights)], rest[len(rights) + 1 : -1], rest[-1]
        n = pl.program_id(0)

        @pl.when(n == 0)
        def _():
            acc[...] = jnp.zeros_like(acc)
            for t, r in enumerate(r_in):

                @pl.when(sel_ref[0] == t)
                def _():
                    pltpu.sync_copy(r, r_ref)

        at = pl.ds(pl.multiple_of(n * chunk, chunk), chunk)
        acc[0:seqs, at] = dot(g_ref[...], r_ref[...], NT).T

        @pl.when(n == pl.num_programs(0) - 1)
        def _():
            send_pieces(me_ref[0], acc, outs)

    return call(
        kernel,
        "grad_left_side",
        (wide // chunk,),
        [pl.BlockSpec((chunk, c_wide), lambda n, *_: (n, 0))]
        + [pl.BlockSpec(memory_space=pl.ANY)] * len(rights),
        [(whole((seqs, c_wide)), kept((seqs, c_wide)))]
        + [(whole((piece_rows, wide)), sent((piece_rows, wide)))] * pieces,
        [pltpu.VMEM((piece_rows * pieces, wide), F32)],
        (sel, me),
        (*near(grad_outer), *rights),
        2e9,
        9e6,
        VMEM // 2,
    )


def tokens(me, cov_t, stat, lefts, rights, normed):
    half, rows, chans = normed.shape[1:]
    seqs = 2 * half
    piece_rows, wide = lefts[0].shape
    narrow = wide // rows
    count = piece_rows * rows
    h = count // 2
    quad = 4 * rows
    last = seqs // piece_rows - 1
    per_half = (last + 1) // 2
    n_l, n_r = len(lefts), len(rights)
    nar2 = 2 * narrow

    def kernel(me_ref, cov_ref, stat_ref, n_ref, *rest):
        l_in = rest[:n_l]
        r_in = rest[n_l : n_l + n_r]
        out, z, t = rest[n_l + n_r :]
        plain = []
        base = (me_ref[0] * piece_rows).astype(F32)
        left = sum(ref[...].astype(F32) for ref in l_in)
        right = sum(ref[...].astype(F32) for ref in r_in)
        drow = depth_rows(cov_ref[...], 128)
        seq = lax.broadcasted_iota(jnp.int32, (piece_rows, narrow), 0).astype(F32) + base
        seq2 = lax.broadcasted_iota(jnp.int32, (piece_rows, 2 * rows), 0).astype(F32) + base
        on = seq2 < depth_lanes(cov_ref[...])
        for i in range(rows):
            v = jnp.where(
                seq < drow[i : i + 1, :narrow], left[:, i * narrow : (i + 1) * narrow], 0.0
            )
            z[pl.ds(i, piece_rows, stride=rows), 0:narrow] = v
        for dp in range(narrow // 2):
            v = jnp.where(on, right[:, dp * 2 * rows : (dp + 1) * 2 * rows], 0.0)
            t[pl.ds(2 * dp, piece_rows, stride=narrow), :] = v[:, :rows]
            t[pl.ds(2 * dp + 1, piece_rows, stride=narrow), :] = v[:, rows:]
        per = 128 // narrow
        for q in range(piece_rows // per):
            tr = t[q * 128 : (q + 1) * 128, :].T
            for k in range(per):
                s = q * per + k
                z[s * rows : (s + 1) * rows, narrow:nar2] = tr[:, k * narrow : (k + 1) * narrow]
        for b in range(piece_rows // 8):
            at = b * 2 * quad
            stats = stat_ref[0, b]
            pair_up, scaled = [], []
            for h2 in range(2):
                v = z[at + h2 * quad : at + (h2 + 1) * quad, :]
                inv = [
                    jnp.broadcast_to(stats[:, 4 * h2 + j : 4 * h2 + j + 1], (rows, nar2))
                    for j in range(4)
                ]
                pair_up.append(v)
                scaled.append(v * jnp.concatenate(inv, axis=0))
            out[b * quad : (b + 1) * quad, :] = jnp.concatenate(scaled, axis=1).astype(BF)
            plain.append(jnp.concatenate(pair_up, axis=1).astype(BF))
        v = jnp.concatenate(plain, axis=0)
        nb = n_ref[...].reshape(piece_rows // 8, 2, quad, chans)
        top = dot(v, nb[:, 0].reshape(h, chans), TN)
        bot = dot(v, nb[:, 1].reshape(h, chans), TN)
        grads = (top[:nar2] + bot[nar2:]).astype(BF)
        for k in range(chans // 128):
            out[h + k * nar2 : h + (k + 1) * nar2, :] = grads[:, k * 128 : (k + 1) * 128]

    return call(
        kernel,
        "tokens",
        (1,),
        [
            whole(cov_t.shape),
            pl.BlockSpec(
                (1, piece_rows // 8, rows, 128),
                lambda n, me: (
                    jnp.minimum(me[0], last) // per_half,
                    jnp.minimum(me[0], last) % per_half,
                    0,
                    0,
                ),
            ),
            pl.BlockSpec(
                (1, piece_rows, rows, chans),
                lambda n, me: (
                    jnp.minimum(me[0], last) // per_half,
                    jnp.minimum(me[0], last) % per_half,
                    0,
                    0,
                ),
            ),
        ]
        + [whole((piece_rows, wide))] * (n_l + n_r),
        [(whole((h + nar2 * chans // 128, 128)), shape((h + nar2 * chans // 128, 128)))],
        [pltpu.VMEM((count, nar2), F32), pltpu.VMEM((piece_rows * narrow, rows), F32)],
        (me,),
        (*far(cov_t, stat, normed, lefts[0]), *lefts[1:], *rights),
        4e8,
        2e6,
        VMEM // 2,
    )[0]


def cut(me, parts, pieces):
    m, lanes = parts[0].shape

    def kernel(me_ref, *rest):
        ins, outs, acc = rest[: len(parts)], rest[len(parts) : -1], rest[-1]
        acc[...] = sum(ref[...].astype(F32) for ref in ins)
        send_pieces(me_ref[0], acc, outs)

    return call(
        kernel,
        "cut",
        (1,),
        [whole((m, lanes))] * len(parts),
        [(whole((m // pieces, lanes)), shape((m // pieces, lanes), F32))] * pieces,
        [pltpu.VMEM((m, lanes), F32)],
        (me,),
        (*far(parts[0]), *parts[1:]),
        1e6,
        1e6,
        VMEM // 2,
    )


def finish(me, qs, xhat, wl_t, wr_t, gain, first, count, before=None):
    _, per_half, rows, chans = xhat.shape
    seqs = 2 * per_half
    pieces = len(qs)
    quad = 4 * rows
    nar2 = 2 * wl_t.shape[0]
    blocks = (qs[0].shape[0] - nar2 * chans // 128) // quad
    per_half //= 8 * blocks
    every = count == 2 * per_half
    given = () if before is None else (before,)

    def piece(n, me_ref):
        return n if every else me_ref[0] ^ (n + first)

    def kernel(me_ref, x_ref, wl_ref, wr_ref, gain_ref, *rest):
        q_in, (out, wc, q_now) = rest[:pieces], rest[-3:]
        n = pl.program_id(0)

        @pl.when(n == 0)
        def _():
            w = jnp.concatenate([wl_ref[...], wr_ref[...]], axis=0).astype(F32) * gain_ref[...]
            w = w - jnp.mean(w, axis=1, keepdims=True)
            hi = w.astype(BF)
            lo = (w - hi.astype(F32)).astype(BF)
            none = jnp.zeros_like(hi)
            wc[0] = jnp.concatenate([hi, none, lo, none], axis=0)
            wc[1] = jnp.concatenate([none, hi, none, lo], axis=0)

        t = piece(n, me_ref) ^ me_ref[0]
        for k in range(pieces):

            @pl.when(t == k)
            def _():
                q_now[...] = q_in[k][0 : blocks * quad, :]

        for b in range(blocks):
            q = q_now[b * quad : (b + 1) * quad, :]
            both = jnp.concatenate([q, q], axis=1)
            for half in range(2):
                g = dot(both, wc[half])
                for j in range(4):
                    s = half * 4 + j
                    xh = x_ref[0, 8 * b + s].astype(F32)
                    gc = g[j * rows : (j + 1) * rows]
                    m = jnp.mean(gc * xh, axis=-1, keepdims=True)
                    out[8 * b + s] = (gc - xh * m).astype(BF)

    blk = pl.BlockSpec((8 * blocks, rows, chans), lambda n, me_ref: (piece(n, me_ref), 0, 0))
    source = pl.BlockSpec(
        (1, 8 * blocks, rows, chans),
        lambda n, me_ref: (piece(n, me_ref) // per_half, piece(n, me_ref) % per_half, 0, 0),
    )
    return pl.pallas_call(
        kernel,
        name="finish",
        grid_spec=pltpu.PrefetchScalarGridSpec(
            num_scalar_prefetch=1,
            grid=(count,),
            in_specs=[
                source,
                whole(wl_t.shape),
                whole(wr_t.shape),
                whole((1, chans)),
            ]
            + [whole(qs[0].shape)] * pieces
            + [pl.BlockSpec(memory_space=pl.ANY)] * len(given),
            out_specs=blk,
            scratch_shapes=[
                pltpu.VMEM((2, 4 * nar2, chans), BF),
                pltpu.VMEM((blocks * quad, 128), BF),
            ],
        ),
        out_shape=sent((seqs, rows, chans)),
        input_output_aliases={5 + pieces: 0} if given else {},
        compiler_params=params(VMEM // 2),
        cost_estimate=pl.CostEstimate(
            flops=int(COST.get("finish_a" if before is None else "finish_b", 0) * 1e9),
            bytes_accessed=1024,
            transcendentals=0,
        ),
    )(me, *near(xhat), *far(wl_t, wr_t, gain[None, :]), *qs, *given)


def join_send(me, parts, qs, nar2):
    m, lanes = parts[0].shape
    n = len(parts)
    extra = nar2 * lanes // 128
    h = qs[0].shape[0] - extra

    def kernel(me_ref, *rest):
        ins, q_in, out, acc = rest[:n], rest[n:-2], rest[-2], rest[-1]
        for t in range(n):
            p = lax.rem(me_ref[0] - t + n, n)
            acc[rows_at(p, m), :] = ins[t][...]
        total = sum(q[...].astype(F32) for q in q_in)
        g = jnp.concatenate(
            [total[k * nar2 : (k + 1) * nar2] for k in range(lanes // 128)], axis=1
        )
        out[0 : n * m, :] = acc[...].astype(BF)
        out[n * m :, :] = g.astype(BF)

    total = n * m + nar2
    return call(
        kernel,
        "join_send",
        (1,),
        [whole((m, lanes))] * n
        + [pl.BlockSpec((extra, 128), lambda *_: (h // extra, 0))] * len(qs),
        [(whole((total, lanes)), sent((total, lanes)))],
        [pltpu.VMEM((n * m, lanes), F32)],
        (me,),
        (*parts, *qs),
        1e6,
        1e6,
        VMEM // 2,
    )[0]


def join_out(me, parts, nar2, narrow):
    rows, lanes = parts[0].shape
    n = len(parts)
    m = rows - nar2
    pair = lanes // 2
    dps = m // narrow

    def kernel(me_ref, *rest):
        ins, (out, lg, rg) = rest[:n], rest[n:]
        for t in range(n):
            p = lax.rem(me_ref[0] - t + n, n)
            v = ins[t][0:m, :].astype(F32)
            for k in range(dps):
                for d2 in range(2):
                    out[pl.ds(2 * (p * dps + k) + d2, narrow, stride=narrow), :] = v[
                        k * narrow : (k + 1) * narrow, d2 * pair : (d2 + 1) * pair
                    ]
        grads = sum(ref[m:, :].astype(F32) for ref in ins)
        lg[...] = grads[:narrow]
        rg[...] = grads[narrow:]

    return call(
        kernel,
        "join_out",
        (1,),
        [whole((rows, lanes))] * n,
        [
            (whole((n * m * 2, pair)), shape((n * m * 2, pair), F32)),
            (whole((narrow, lanes)), shape((narrow, lanes), F32)),
            (whole((narrow, lanes)), shape((narrow, lanes), F32)),
        ],
        [],
        (me,),
        (*far(parts[0]), *parts[1:]),
        1e6,
        1e6,
        VMEM // 2,
    )


BOTH = ("row", "col")


def shift(value, axis, t):
    n = lax.axis_size(axis)
    return lax.ppermute(value, axis, [(k, (k + t) % n) for k in range(n)])


def shifts(own, others, axis):
    return [own] + [shift(v, axis, t + 1) for t, v in enumerate(others)]


def swap(value, axis, t):
    n = lax.axis_size(axis)
    return lax.ppermute(value, axis, [(k, k ^ t) for k in range(n)])


def gather(value, axis):
    n = lax.axis_size(axis)
    if n == 4:
        near, far = swap(value, axis, 1), swap(value, axis, 2)
        return [value, near, far, swap(far, axis, 1)]
    return [value] + [swap(value, axis, t) for t in range(1, n)]


def spread_small(value, m, ratio):
    n_row, n_col = lax.axis_size("row"), lax.axis_size("col")
    total = None
    for first in range(1, n_row, n_col - 1):
        pairs = []
        for c in range(n_col):
            b = c * ratio + m
            for k, t in enumerate(range(first, min(first + n_col - 1, n_row))):
                pairs.append((b * n_col + (c + 1 + k) % n_col, (b + t) % n_row * n_col + c))
        got = lax.ppermute(value, BOTH, pairs)
        total = got if total is None else total + got
    return total


def spread(value, m, ratio):
    n_row, n_col = lax.axis_size("row"), lax.axis_size("col")
    out = [value]
    if n_row == 4 and n_col == 4:
        first = [(c * n_col + c, (c ^ 2) * n_col + c) for c in range(n_col)]
        first += [(c * n_col + (c ^ 1), (c ^ 1) * n_col + c) for c in range(n_col)]
        second = [(c * n_col + c, (c ^ 3) * n_col + c) for c in range(n_col)]
        return [value, lax.ppermute(value, BOTH, first), lax.ppermute(value, BOTH, second)]
    for t in range(1, n_row):
        pairs = [
            ((c * ratio + m) * n_col + c, (c * ratio + m + t) % n_row * n_col + c)
            for c in range(n_col)
        ]
        out.append(lax.ppermute(value, BOTH, pairs))
    return out


def spread_choice(row, col, m, ratio):
    n_row, n_col = lax.axis_size("row"), lax.axis_size("col")
    if n_row == 4 and n_col == 4:
        apart = row ^ col
        return jnp.where(apart == 3, 2, jnp.where(apart == 0, 0, 1))
    return (row - (col * ratio + m) + n_row) % n_row


def to_owners(pieces, ratio):
    n_row, n_col = lax.axis_size("row"), lax.axis_size("col")
    row = lax.axis_index("row")
    if ratio > 1:
        stacked = jnp.stack(pieces)
        pieces = [
            lax.dynamic_index_in_dim(stacked, (row + t) % n_row, 0, keepdims=False)
            for t in range(n_row)
        ]
    parts = []
    for t, piece in enumerate(pieces):
        pairs = []
        for r in range(n_row):
            m, k = divmod((r + t) % n_row, n_col)
            pairs += [(r * n_col + c, (c * ratio + m) * n_col + k) for c in range(n_col)]
        parts.append(lax.ppermute(piece, BOTH, pairs))
    return parts


def one(value):
    return value[None].astype(jnp.int32)


def body(
    alignment,
    coverage,
    layer_norm_gain,
    layer_norm_bias,
    left_weight,
    right_weight,
    out_weight,
    out_bias,
    cotangent,
):
    n_row, n_col = lax.axis_size("row"), lax.axis_size("col")
    ratio = n_row // n_col
    row_index = lax.axis_index("row")
    col_index = lax.axis_index("col")
    me_row, me_col = one(row_index), one(col_index)
    seqs, rows, chans = alignment.shape
    narrow = left_weight.shape[1]
    pair = out_weight.shape[1]
    piece_rows = (seqs // n_col + 7) // 8 * 8
    cov_t = coverage.T
    wl_t, wr_t = left_weight.T, right_weight.T

    cov_far = [spread_small(cov_t, m, ratio) for m in range(ratio)]
    normed, xhat, stat, right = project(cov_t, alignment, layer_norm_gain, layer_norm_bias, wr_t)
    right, cov_far = lax.optimization_barrier((right, cov_far))

    right_pieces, firsts = [], []
    for m in range(ratio):
        own = one(row_index == col_index * ratio + m)
        turn_by = one(row_index) if ratio == 1 else jnp.zeros_like(me_row)
        scaled, grad_outer, w2, left_t, dcol, *pieces = right_side(
            own,
            turn_by,
            cov_t,
            cov_far[m],
            cotangent,
            out_weight,
            wl_t,
            normed,
            m,
            n_col,
            piece_rows,
        )
        firsts.append((scaled, grad_outer, w2, left_t, dcol))
        right_pieces.extend(pieces)
    right_parts = to_owners(right_pieces, ratio)

    left_pieces, updates, weight_pieces = None, [], None
    for m in range(ratio):
        scaled, grad_outer, w2, left_t, dcol = firsts[m]
        sel = one(spread_choice(row_index, col_index, m, ratio))
        right_cols, *pieces = left_side(
            sel, me_col, grad_outer, spread(right, m, ratio), n_col, piece_rows
        )
        update, *gw = forward(
            me_row, cov_t, left_t, right_cols, scaled, w2, dcol, out_bias, n_row
        )
        updates.append(update)
        if m == 0:
            left_pieces, weight_pieces = pieces, gw
        else:
            left_pieces = [(a.astype(F32) + b).astype(BF) for a, b in zip(left_pieces, pieces)]
            weight_pieces = [
                (a.astype(F32) + b).astype(a.dtype) for a, b in zip(weight_pieces, gw)
            ]
    pair_update = updates[0] if ratio == 1 else jnp.concatenate(updates, axis=1)

    gw_parts = shifts(weight_pieces[0], weight_pieces[1:], "row")
    lefts = shifts(left_pieces[0], left_pieces[1:], "col")
    lefts, pair_update = lax.optimization_barrier((lefts, pair_update))
    q = tokens(me_col, cov_t, stat, lefts, right_parts, normed)
    qs = gather(q, "col")

    if weight_pieces[0].shape[0] % (8 * n_col) == 0:
        pieces = cut(me_col, gw_parts, n_col)
        part = sum(shifts(pieces[0], pieces[1:], "col"))
        parts = [part] + [shift(part, "col", t) for t in range(1, n_col)]
    else:
        parts = [lax.psum(cut(me_col, gw_parts, 1)[0], "col")]
    ends = (xhat, wl_t, wr_t, layer_norm_gain)
    if n_col == 4:
        gradient = finish(me_col, [qs[0], qs[1]], *ends, 0, 2)
        gradient, parts = lax.optimization_barrier((gradient, parts))
    last = join_send(me_col, parts, qs, 2 * narrow)
    lasts = [last] + [shift(last, "row", t) for t in range(1, n_row)]
    if n_col == 4:
        gradient = finish(me_col, qs, *ends, 2, 2, gradient)
    else:
        gradient = finish(me_col, qs, *ends, 0, seqs // piece_rows)
    lasts, gradient = lax.optimization_barrier((lasts, gradient))
    grad_out, grad_left, grad_right = join_out(me_row, lasts, 2 * narrow, narrow)
    return pair_update, gradient, grad_left.T, grad_right.T, grad_out


def solution(mesh):
    return jax.shard_map(
        body,
        mesh=mesh,
        in_specs=(
            P("grp", "row", None),
            P("grp", "row"),
            P(),
            P(),
            P(),
            P(),
            P(),
            P(),
            P(("grp", "row"), "col", None),
        ),
        out_specs=(
            P(("grp", "row"), "col", None),
            P("grp", "row", None),
            P("grp", None),
            P("grp", None),
            P("grp", None),
        ),
        check_vma=False,
    )
```

```python
import jax
import jax.numpy as jnp
from jax import lax
from jax.experimental import pallas as pl
from jax.experimental.pallas import tpu as pltpu
from jax.sharding import PartitionSpec as P

BF = jnp.bfloat16
F32 = jnp.float32
NN = (((1,), (0,)), ((), ()))
NT = (((1,), (1,)), ((), ()))
TN = (((0,), (0,)), ((), ()))
VMEM = 64 * 1024 * 1024
COST = {'grad_outer_right': 4, 'grad_left_side': 4, 'cut': 20, 'finish_a': 2, 'finish_b': 6, 'join_send': 2, 'project': 1}
IBLK = 32


def params(vmem=VMEM):
    return pltpu.CompilerParams(vmem_limit_bytes=vmem)


def dot(a, b, dims=NN):
    return lax.dot_general(a, b, dims, preferred_element_type=F32)


def whole(shape):
    return pl.BlockSpec(shape, lambda *_: (0,) * len(shape))


def shape(dims, dtype=BF):
    return jax.ShapeDtypeStruct(dims, dtype)


def far(*values):
    return tuple(pltpu.with_memory_space_constraint(v, pltpu.HBM) for v in values)


def near(*values):
    return tuple(pltpu.with_memory_space_constraint(v, pltpu.VMEM) for v in values)


def sent(dims, dtype=BF):
    return pltpu.HBM(dims, dtype)


def kept(dims, dtype=BF):
    return pltpu.VMEM(dims, dtype)


def call(
    kernel, name, grid, ins, outs, scratch, scalars, arrays, flops, bytes_accessed, vmem=VMEM
):
    return pl.pallas_call(
        kernel,
        name=name,
        grid_spec=pltpu.PrefetchScalarGridSpec(
            num_scalar_prefetch=len(scalars),
            grid=grid,
            in_specs=ins,
            out_specs=[o[0] for o in outs],
            scratch_shapes=scratch,
        ),
        out_shape=[o[1] for o in outs],
        compiler_params=params(vmem),
        cost_estimate=pl.CostEstimate(
            flops=int(COST.get(name, 0) * 1e9), bytes_accessed=1024, transcendentals=0
        ),
    )(*scalars, *arrays)


def depth_rows(cov, lanes):
    total = jnp.sum(cov.astype(F32), axis=1, keepdims=True)
    return jnp.broadcast_to(total, (cov.shape[0], lanes))


def depth_lanes(cov):
    row = depth_rows(cov, cov.shape[0]).T[0:1, :]
    return jnp.concatenate([row, row], axis=1)


def project(cov_t, alignment, gain, bias, wr_t):
    seqs, rows, chans = alignment.shape
    narrow = wr_t.shape[0]
    half = seqs // 2
    blk = 16
    steps = half // blk
    wide = rows * narrow

    def kernel(
        cov_ref, x_ref, gain_ref, bias_ref, w_ref, normed_ref, xhat_ref, stat_ref, r_ref, ys, nbs
    ):
        n = pl.program_id(0)
        gain_v = gain_ref[...]
        bias_v = bias_ref[...]
        lane = lax.broadcasted_iota(jnp.int32, (rows, 128), 1)
        for s2 in range(2):
            for g in range(blk):
                if g % 8 == 0:
                    stat = jnp.zeros((rows, 128), F32)
                x = x_ref[s2, g].astype(F32)
                mean = jnp.mean(x, axis=-1, keepdims=True)
                c = x - mean
                inv = lax.rsqrt(jnp.mean(c * c, axis=-1, keepdims=True) + 1e-05)
                xhat = c * inv
                nb = (xhat * gain_v + bias_v).astype(BF)
                normed_ref[s2, g] = nb
                xhat_ref[s2, g] = xhat.astype(BF)
                at = (2 * g + s2) * rows
                nbs[at : at + rows, :] = nb
                stat = jnp.where(lane == g % 8, inv, stat)
                stat_ref[s2, g // 8] = stat
        y = dot(w_ref[...], nbs[...], NT)
        for g in range(blk):
            at = (n * blk + g) * narrow
            ys[pl.ds(pl.multiple_of(at, narrow), narrow), :] = y[
                :, g * 2 * rows : (g + 1) * 2 * rows
            ]

        @pl.when(n == steps - 1)
        def _():
            lanes = lax.broadcasted_iota(jnp.int32, (half, 2 * rows), 1)
            seq = lax.broadcasted_iota(jnp.int32, (half, 2 * rows), 0).astype(F32)
            low = lanes < rows
            dep = depth_lanes(cov_ref[...])
            top_on = seq < dep
            bot_on = seq + half < dep
            for dp in range(narrow // 2):
                even = ys[pl.ds(2 * dp, half, stride=narrow), :]
                odd = ys[pl.ds(2 * dp + 1, half, stride=narrow), :]
                top = jnp.where(low, even, pltpu.roll(odd, rows, 1))
                bot = jnp.where(low, pltpu.roll(even, rows, 1), odd)
                at = slice(dp * 2 * rows, (dp + 1) * 2 * rows)
                r_ref[0:half, at] = jnp.where(top_on, top, 0.0).astype(BF)
                r_ref[half : 2 * half, at] = jnp.where(bot_on, bot, 0.0).astype(BF)

    tile = pl.BlockSpec((2, blk, rows, chans), lambda n: (0, n, 0, 0))
    return call(
        kernel,
        "project",
        (steps,),
        [
            whole(cov_t.shape),
            tile,
            whole((1, chans)),
            whole((1, chans)),
            whole(wr_t.shape),
        ],
        [
            (tile, sent((2, half, rows, chans))),
            (tile, sent((2, half, rows, chans))),
            (
                pl.BlockSpec((2, blk // 8, rows, 128), lambda n: (0, n, 0, 0)),
                sent((2, half // 8, rows, 128), F32),
            ),
            (whole((seqs, wide)), sent((seqs, wide))),
        ],
        [
            pltpu.VMEM((half * narrow, 2 * rows), F32),
            pltpu.VMEM((2 * blk * rows, chans), BF),
        ],
        (),
        far(
            cov_t,
            alignment.reshape(2, half, rows, chans),
            gain[None, :],
            bias[None, :],
            wr_t,
        ),
        2e9,
        7e6,
        VMEM // 2,
    )


def pair_block(a, b):
    z = jnp.zeros_like(a)
    return jnp.concatenate(
        [
            jnp.concatenate([a, z], axis=1),
            jnp.concatenate([z, a], axis=1),
            jnp.concatenate([b, z], axis=1),
            jnp.concatenate([z, b], axis=1),
        ],
        axis=0,
    )


def rows_at(p, count):
    start = p * count
    if count % 8 == 0:
        start = pl.multiple_of(start, 8)
    return pl.ds(start, count)


def send_pieces(me, acc, outs):
    rows = outs[0].shape[0]
    count = len(outs)
    for t, out in enumerate(outs):
        p = lax.rem(me + t, count)
        out[...] = acc[rows_at(p, rows), :].astype(out.dtype)


def right_side(own, me, cov_t, cov_far, cot, out_weight, wl_t, normed, block, pieces, piece_rows):
    rows, _, pair = cot.shape
    half, chans = normed.shape[1], normed.shape[3]
    seqs = 2 * half
    cols = cov_far.shape[0]
    narrow = wl_t.shape[0]
    wide = rows * narrow
    c_wide = cols * narrow
    i_blk = 16

    def kernel(
        own_ref,
        me_ref,
        cov_ref,
        far_ref,
        cot_ref,
        wo_ref,
        wl_ref,
        n_ref,
        s_ref,
        g_ref,
        w2_ref,
        lt_ref,
        dcol,
        *rest,
    ):
        outs = rest[:pieces]
        acc, wide_f, z, drow = rest[pieces:]
        n = pl.program_id(0)

        @pl.when(n == 0)
        def _():
            acc[...] = jnp.zeros_like(acc)
            drow[...] = depth_rows(cov_ref[...], 128)
            mine = (own_ref[0] == 1).astype(F32)
            far = depth_rows(far_ref[...], 128)
            dcol[...] = mine * drow[...] + (1.0 - mine) * far
            wide_f[...] = wo_ref[...].astype(F32)
            for dp in range(narrow // 2):
                for d2 in range(2):
                    v = wide_f[pl.ds(2 * dp + d2, narrow, stride=narrow), :]
                    w2_ref[dp * narrow : (dp + 1) * narrow, d2 * pair : (d2 + 1) * pair] = (
                        v.astype(BF)
                    )

        dep = dcol[...]
        w = w2_ref[...]
        mine_rows = drow[pl.ds(pl.multiple_of(n * i_blk, i_blk), i_blk), :]
        blk = n_ref[...].astype(F32).reshape(seqs * i_blk, chans).astype(BF)
        z[...] = dot(blk, wl_ref[...], NT)
        seq = lax.broadcasted_iota(jnp.int32, (seqs, narrow), 0).astype(F32)
        per = 128 // narrow
        tiles = []
        for q in range(i_blk // per):
            parts = []
            for k in range(per):
                i = q * per + k
                v = z[pl.ds(i, seqs, stride=i_blk), :]
                parts.append(jnp.where(seq < mine_rows[i : i + 1, :narrow], v, 0.0))
            tile = jnp.concatenate(parts, axis=1)
            lt_ref[q * 128 : (q + 1) * 128, :] = tile.T.astype(BF)
            tiles.append(tile.astype(BF))
        left = jnp.concatenate(tiles, axis=1)
        for ip in range(i_blk // 2):
            scaled = []
            for k in range(2):
                i = 2 * ip + k
                den = jnp.maximum(jnp.minimum(dep, mine_rows[i : i + 1, :]), 1.0)
                s = (cot_ref[i].astype(F32) / den).astype(BF)
                s_ref[i] = s
                scaled.append(s)
            g = dot(w, pair_block(*scaled), NT).astype(BF)
            for k in range(2):
                i = 2 * ip + k
                for dp in range(narrow // 2):
                    g_ref[
                        i * narrow : (i + 1) * narrow, dp * 2 * cols : (dp + 1) * 2 * cols
                    ] = g[dp * narrow : (dp + 1) * narrow, k * 2 * cols : (k + 1) * 2 * cols]
        acc[0:seqs, :] += dot(left, g_ref[...])

        @pl.when(n == pl.num_programs(0) - 1)
        def _():
            send_pieces(me_ref[0], acc, outs)

    return call(
        kernel,
        "grad_outer_right",
        (rows // i_blk,),
        [
            whole(cov_t.shape),
            whole(cov_far.shape),
            pl.BlockSpec((i_blk, cols, pair), lambda n, *_: (n, block, 0)),
            whole(out_weight.shape),
            whole(wl_t.shape),
            pl.BlockSpec((2, half, i_blk, chans), lambda n, *_: (0, 0, n, 0)),
        ],
        [
            (
                pl.BlockSpec((i_blk, cols, pair), lambda n, *_: (n, 0, 0)),
                kept((rows, cols, pair)),
            ),
            (pl.BlockSpec((i_blk * narrow, c_wide), lambda n, *_: (n, 0)), kept((wide, c_wide))),
            (
                whole((narrow * narrow // 2, 2 * pair)),
                kept((narrow * narrow // 2, 2 * pair)),
            ),
            (pl.BlockSpec((i_blk * narrow, seqs), lambda n, *_: (n, 0)), kept((wide, seqs))),
            (whole((cols, 128)), kept((cols, 128), F32)),
        ]
        + [(whole((piece_rows, c_wide)), sent((piece_rows, c_wide)))] * pieces,
        [
            pltpu.VMEM((piece_rows * pieces, c_wide), F32),
            pltpu.VMEM(out_weight.shape, F32),
            pltpu.VMEM((seqs * i_blk, narrow), F32),
            pltpu.VMEM((rows, 128), F32),
        ],
        (own, me),
        (*far(cov_t), *near(cov_far), *far(cot, out_weight, wl_t, normed)),
        4e9,
        16e6,
        VMEM // 2,
    )


def forward(me, cov_t, left_t, right, scaled, w2, dcol, bias, pieces):
    rows, cols, pair = scaled.shape
    wide, seqs = left_t.shape
    narrow = wide // rows
    c_wide = cols * narrow
    i_blk = IBLK
    high = narrow * narrow // 2
    part = high // pieces

    def kernel(
        me_ref, cov_ref, lt_ref, r_ref, s_ref, w2_ref, dcol_ref, bias_ref, pu_ref, *rest
    ):
        outs = rest[:-3]
        acc, w2t, drow = rest[-3:]
        n = pl.program_id(0)

        @pl.when(n == 0)
        def _():
            acc[...] = jnp.zeros_like(acc)
            w2t[...] = w2_ref[...].astype(F32).T.astype(BF)
            drow[...] = depth_rows(cov_ref[...], 128)

        lane = lax.broadcasted_iota(jnp.int32, (pair, 2 * cols), 1)
        low = lane < cols
        dep = dcol_ref[...]
        mine_rows = drow[pl.ds(pl.multiple_of(n * i_blk, i_blk), i_blk), :]
        outer = dot(lt_ref[...], r_ref[...]).astype(BF)
        x = jnp.concatenate(
            [
                jnp.concatenate(
                    [
                        outer[
                            i * narrow : (i + 1) * narrow, dp * 2 * cols : (dp + 1) * 2 * cols
                        ]
                        for dp in range(narrow // 2)
                    ],
                    axis=0,
                )
                for i in range(i_blk)
            ],
            axis=1,
        )
        sbd = jnp.concatenate(
            [pair_block(s_ref[2 * k], s_ref[2 * k + 1]) for k in range(i_blk // 2)], axis=0
        )
        acc[...] += dot(x, sbd)
        pt = dot(w2t[...], x)
        for ip in range(i_blk // 2):
            at = ip * 4 * cols
            e0, o0 = pt[:pair, at : at + 2 * cols], pt[:pair, at + 2 * cols : at + 4 * cols]
            e1, o1 = pt[pair:, at : at + 2 * cols], pt[pair:, at + 2 * cols : at + 4 * cols]
            both = jnp.where(low, e0, o1) + pltpu.roll(jnp.where(low, o0, e1), cols, 1)
            both = both.T + bias_ref[...]
            for k in range(2):
                i = 2 * ip + k
                den = jnp.maximum(jnp.minimum(dep, mine_rows[i : i + 1, :]), 1.0)
                pu_ref[i] = (both[k * cols : (k + 1) * cols] / den).astype(BF)

        @pl.when(n == pl.num_programs(0) - 1)
        def _():
            send_pieces(me_ref[0], acc, outs)

    return call(
        kernel,
        "forward",
        (rows // i_blk,),
        [
            whole(cov_t.shape),
            pl.BlockSpec((i_blk * narrow, seqs), lambda n, *_: (n, 0)),
            whole(right.shape),
            pl.BlockSpec((i_blk, cols, pair), lambda n, *_: (n, 0, 0)),
            whole(w2.shape),
            whole(dcol.shape),
            whole((1, pair)),
        ],
        [
            (
                pl.BlockSpec((i_blk, cols, pair), lambda n, *_: (n, 0, 0)),
                sent((rows, cols, pair)),
            ),
            (whole((part, 2 * pair)), sent((part, 2 * pair), F32)),
        ]
        + [(whole((part, 2 * pair)), sent((part, 2 * pair)))] * (pieces - 1),
        [
            pltpu.VMEM((high, 2 * pair), F32),
            pltpu.VMEM((w2.shape[1], w2.shape[0]), BF),
            pltpu.VMEM((rows, 128), F32),
        ],
        (me,),
        (*far(cov_t), *near(left_t, right, scaled, w2, dcol), *far(bias[None, :])),
        6e9,
        6e6,
        VMEM // 2,
    )


def left_side(sel, me, grad_outer, rights, pieces, piece_rows):
    wide, c_wide = grad_outer.shape
    seqs = rights[0].shape[0]
    chunk = 512

    def kernel(sel_ref, me_ref, g_ref, *rest):
        r_in = rest[: len(rights)]
        r_ref, outs, acc = rest[len(rights)], rest[len(rights) + 1 : -1], rest[-1]
        n = pl.program_id(0)

        @pl.when(n == 0)
        def _():
            acc[...] = jnp.zeros_like(acc)
            for t, r in enumerate(r_in):

                @pl.when(sel_ref[0] == t)
                def _():
                    pltpu.sync_copy(r, r_ref)

        at = pl.ds(pl.multiple_of(n * chunk, chunk), chunk)
        acc[0:seqs, at] = dot(g_ref[...], r_ref[...], NT).T

        @pl.when(n == pl.num_programs(0) - 1)
        def _():
            send_pieces(me_ref[0], acc, outs)

    return call(
        kernel,
        "grad_left_side",
        (wide // chunk,),
        [pl.BlockSpec((chunk, c_wide), lambda n, *_: (n, 0))]
        + [pl.BlockSpec(memory_space=pl.ANY)] * len(rights),
        [(whole((seqs, c_wide)), kept((seqs, c_wide)))]
        + [(whole((piece_rows, wide)), sent((piece_rows, wide)))] * pieces,
        [pltpu.VMEM((piece_rows * pieces, wide), F32)],
        (sel, me),
        (*near(grad_outer), *rights),
        2e9,
        9e6,
        VMEM // 2,
    )


def tokens(me, cov_t, stat, lefts, rights, normed):
    half, rows, chans = normed.shape[1:]
    seqs = 2 * half
    piece_rows, wide = lefts[0].shape
    narrow = wide // rows
    count = piece_rows * rows
    h = count // 2
    quad = 4 * rows
    last = seqs // piece_rows - 1
    per_half = (last + 1) // 2
    n_l, n_r = len(lefts), len(rights)
    nar2 = 2 * narrow

    def kernel(me_ref, cov_ref, stat_ref, n_ref, *rest):
        l_in = rest[:n_l]
        r_in = rest[n_l : n_l + n_r]
        out, z, t = rest[n_l + n_r :]
        plain = []
        base = (me_ref[0] * piece_rows).astype(F32)
        left = sum(ref[...].astype(F32) for ref in l_in)
        right = sum(ref[...].astype(F32) for ref in r_in)
        drow = depth_rows(cov_ref[...], 128)
        seq = lax.broadcasted_iota(jnp.int32, (piece_rows, narrow), 0).astype(F32) + base
        seq2 = lax.broadcasted_iota(jnp.int32, (piece_rows, 2 * rows), 0).astype(F32) + base
        on = seq2 < depth_lanes(cov_ref[...])
        for i in range(rows):
            v = jnp.where(
                seq < drow[i : i + 1, :narrow], left[:, i * narrow : (i + 1) * narrow], 0.0
            )
            z[pl.ds(i, piece_rows, stride=rows), 0:narrow] = v
        for dp in range(narrow // 2):
            v = jnp.where(on, right[:, dp * 2 * rows : (dp + 1) * 2 * rows], 0.0)
            t[pl.ds(2 * dp, piece_rows, stride=narrow), :] = v[:, :rows]
            t[pl.ds(2 * dp + 1, piece_rows, stride=narrow), :] = v[:, rows:]
        per = 128 // narrow
        for q in range(piece_rows // per):
            tr = t[q * 128 : (q + 1) * 128, :].T
            for k in range(per):
                s = q * per + k
                z[s * rows : (s + 1) * rows, narrow:nar2] = tr[:, k * narrow : (k + 1) * narrow]
        for b in range(piece_rows // 8):
            at = b * 2 * quad
            stats = stat_ref[0, b]
            pair_up, scaled = [], []
            for h2 in range(2):
                v = z[at + h2 * quad : at + (h2 + 1) * quad, :]
                inv = [
                    jnp.broadcast_to(stats[:, 4 * h2 + j : 4 * h2 + j + 1], (rows, nar2))
                    for j in range(4)
                ]
                pair_up.append(v)
                scaled.append(v * jnp.concatenate(inv, axis=0))
            out[b * quad : (b + 1) * quad, :] = jnp.concatenate(scaled, axis=1).astype(BF)
            plain.append(jnp.concatenate(pair_up, axis=1).astype(BF))
        v = jnp.concatenate(plain, axis=0)
        nb = n_ref[...].reshape(piece_rows // 8, 2, quad, chans)
        top = dot(v, nb[:, 0].reshape(h, chans), TN)
        bot = dot(v, nb[:, 1].reshape(h, chans), TN)
        grads = (top[:nar2] + bot[nar2:]).astype(BF)
        for k in range(chans // 128):
            out[h + k * nar2 : h + (k + 1) * nar2, :] = grads[:, k * 128 : (k + 1) * 128]

    return call(
        kernel,
        "tokens",
        (1,),
        [
            whole(cov_t.shape),
            pl.BlockSpec(
                (1, piece_rows // 8, rows, 128),
                lambda n, me: (
                    jnp.minimum(me[0], last) // per_half,
                    jnp.minimum(me[0], last) % per_half,
                    0,
                    0,
                ),
            ),
            pl.BlockSpec(
                (1, piece_rows, rows, chans),
                lambda n, me: (
                    jnp.minimum(me[0], last) // per_half,
                    jnp.minimum(me[0], last) % per_half,
                    0,
                    0,
                ),
            ),
        ]
        + [whole((piece_rows, wide))] * (n_l + n_r),
        [(whole((h + nar2 * chans // 128, 128)), shape((h + nar2 * chans // 128, 128)))],
        [pltpu.VMEM((count, nar2), F32), pltpu.VMEM((piece_rows * narrow, rows), F32)],
        (me,),
        (*far(cov_t, stat, normed, lefts[0]), *lefts[1:], *rights),
        4e8,
        2e6,
        VMEM // 2,
    )[0]


def cut(me, parts, pieces):
    m, lanes = parts[0].shape

    def kernel(me_ref, *rest):
        ins, outs, acc = rest[: len(parts)], rest[len(parts) : -1], rest[-1]
        acc[...] = sum(ref[...].astype(F32) for ref in ins)
        send_pieces(me_ref[0], acc, outs)

    return call(
        kernel,
        "cut",
        (1,),
        [whole((m, lanes))] * len(parts),
        [(whole((m // pieces, lanes)), shape((m // pieces, lanes), F32))] * pieces,
        [pltpu.VMEM((m, lanes), F32)],
        (me,),
        (*far(parts[0]), *parts[1:]),
        1e6,
        1e6,
        VMEM // 2,
    )


def finish(me, qs, xhat, wl_t, wr_t, gain, first, count, before=None):
    _, per_half, rows, chans = xhat.shape
    seqs = 2 * per_half
    pieces = len(qs)
    quad = 4 * rows
    nar2 = 2 * wl_t.shape[0]
    blocks = (qs[0].shape[0] - nar2 * chans // 128) // quad
    per_half //= 8 * blocks
    every = count == 2 * per_half
    given = () if before is None else (before,)

    def piece(n, me_ref):
        return n if every else me_ref[0] ^ (n + first)

    def kernel(me_ref, x_ref, wl_ref, wr_ref, gain_ref, *rest):
        q_in, (out, wc, q_now) = rest[:pieces], rest[-3:]
        n = pl.program_id(0)

        @pl.when(n == 0)
        def _():
            w = jnp.concatenate([wl_ref[...], wr_ref[...]], axis=0).astype(F32) * gain_ref[...]
            w = w - jnp.mean(w, axis=1, keepdims=True)
            hi = w.astype(BF)
            lo = (w - hi.astype(F32)).astype(BF)
            none = jnp.zeros_like(hi)
            wc[0] = jnp.concatenate([hi, none, lo, none], axis=0)
            wc[1] = jnp.concatenate([none, hi, none, lo], axis=0)

        t = piece(n, me_ref) ^ me_ref[0]
        for k in range(pieces):

            @pl.when(t == k)
            def _():
                q_now[...] = q_in[k][0 : blocks * quad, :]

        for b in range(blocks):
            q = q_now[b * quad : (b + 1) * quad, :]
            both = jnp.concatenate([q, q], axis=1)
            for half in range(2):
                g = dot(both, wc[half])
                for j in range(4):
                    s = half * 4 + j
                    xh = x_ref[0, 8 * b + s].astype(F32)
                    gc = g[j * rows : (j + 1) * rows]
                    m = jnp.mean(gc * xh, axis=-1, keepdims=True)
                    out[8 * b + s] = (gc - xh * m).astype(BF)

    blk = pl.BlockSpec((8 * blocks, rows, chans), lambda n, me_ref: (piece(n, me_ref), 0, 0))
    source = pl.BlockSpec(
        (1, 8 * blocks, rows, chans),
        lambda n, me_ref: (piece(n, me_ref) // per_half, piece(n, me_ref) % per_half, 0, 0),
    )
    return pl.pallas_call(
        kernel,
        name="finish",
        grid_spec=pltpu.PrefetchScalarGridSpec(
            num_scalar_prefetch=1,
            grid=(count,),
            in_specs=[
                source,
                whole(wl_t.shape),
                whole(wr_t.shape),
                whole((1, chans)),
            ]
            + [whole(qs[0].shape)] * pieces
            + [pl.BlockSpec(memory_space=pl.ANY)] * len(given),
            out_specs=blk,
            scratch_shapes=[
                pltpu.VMEM((2, 4 * nar2, chans), BF),
                pltpu.VMEM((blocks * quad, 128), BF),
            ],
        ),
        out_shape=sent((seqs, rows, chans)),
        input_output_aliases={5 + pieces: 0} if given else {},
        compiler_params=params(VMEM // 2),
        cost_estimate=pl.CostEstimate(
            flops=int(COST.get("finish_a" if before is None else "finish_b", 0) * 1e9),
            bytes_accessed=1024,
            transcendentals=0,
        ),
    )(me, *far(xhat, wl_t, wr_t, gain[None, :]), *qs, *given)


def join_send(me, parts, qs, nar2):
    m, lanes = parts[0].shape
    n = len(parts)
    extra = nar2 * lanes // 128
    h = qs[0].shape[0] - extra

    def kernel(me_ref, *rest):
        ins, q_in, out, acc = rest[:n], rest[n:-2], rest[-2], rest[-1]
        for t in range(n):
            p = lax.rem(me_ref[0] - t + n, n)
            acc[rows_at(p, m), :] = ins[t][...]
        total = sum(q[...].astype(F32) for q in q_in)
        g = jnp.concatenate(
            [total[k * nar2 : (k + 1) * nar2] for k in range(lanes // 128)], axis=1
        )
        out[0 : n * m, :] = acc[...].astype(BF)
        out[n * m :, :] = g.astype(BF)

    total = n * m + nar2
    return call(
        kernel,
        "join_send",
        (1,),
        [whole((m, lanes))] * n
        + [pl.BlockSpec((extra, 128), lambda *_: (h // extra, 0))] * len(qs),
        [(whole((total, lanes)), sent((total, lanes)))],
        [pltpu.VMEM((n * m, lanes), F32)],
        (me,),
        (*parts, *qs),
        1e6,
        1e6,
        VMEM // 2,
    )[0]


def join_out(me, parts, nar2, narrow):
    rows, lanes = parts[0].shape
    n = len(parts)
    m = rows - nar2
    pair = lanes // 2
    dps = m // narrow

    def kernel(me_ref, *rest):
        ins, (out, lg, rg) = rest[:n], rest[n:]
        for t in range(n):
            p = lax.rem(me_ref[0] - t + n, n)
            v = ins[t][0:m, :].astype(F32)
            for k in range(dps):
                for d2 in range(2):
                    out[pl.ds(2 * (p * dps + k) + d2, narrow, stride=narrow), :] = v[
                        k * narrow : (k + 1) * narrow, d2 * pair : (d2 + 1) * pair
                    ]
        grads = sum(ref[m:, :].astype(F32) for ref in ins)
        lg[...] = grads[:narrow]
        rg[...] = grads[narrow:]

    return call(
        kernel,
        "join_out",
        (1,),
        [whole((rows, lanes))] * n,
        [
            (whole((n * m * 2, pair)), shape((n * m * 2, pair), F32)),
            (whole((narrow, lanes)), shape((narrow, lanes), F32)),
            (whole((narrow, lanes)), shape((narrow, lanes), F32)),
        ],
        [],
        (me,),
        (*far(parts[0]), *parts[1:]),
        1e6,
        1e6,
        VMEM // 2,
    )


BOTH = ("row", "col")


def shift(value, axis, t):
    n = lax.axis_size(axis)
    return lax.ppermute(value, axis, [(k, (k + t) % n) for k in range(n)])


def shifts(own, others, axis):
    return [own] + [shift(v, axis, t + 1) for t, v in enumerate(others)]


def swap(value, axis, t):
    n = lax.axis_size(axis)
    return lax.ppermute(value, axis, [(k, k ^ t) for k in range(n)])


def gather(value, axis):
    n = lax.axis_size(axis)
    if n == 4:
        near, far = swap(value, axis, 1), swap(value, axis, 2)
        return [value, near, far, swap(far, axis, 1)]
    return [value] + [swap(value, axis, t) for t in range(1, n)]


def spread_small(value, m, ratio):
    n_row, n_col = lax.axis_size("row"), lax.axis_size("col")
    total = None
    for first in range(1, n_row, n_col - 1):
        pairs = []
        for c in range(n_col):
            b = c * ratio + m
            for k, t in enumerate(range(first, min(first + n_col - 1, n_row))):
                pairs.append((b * n_col + (c + 1 + k) % n_col, (b + t) % n_row * n_col + c))
        got = lax.ppermute(value, BOTH, pairs)
        total = got if total is None else total + got
    return total


def spread(value, m, ratio):
    n_row, n_col = lax.axis_size("row"), lax.axis_size("col")
    out = [value]
    if n_row == 4 and n_col == 4:
        first = [(c * n_col + c, (c ^ 2) * n_col + c) for c in range(n_col)]
        first += [(c * n_col + (c ^ 1), (c ^ 1) * n_col + c) for c in range(n_col)]
        second = [(c * n_col + c, (c ^ 3) * n_col + c) for c in range(n_col)]
        return [value, lax.ppermute(value, BOTH, first), lax.ppermute(value, BOTH, second)]
    for t in range(1, n_row):
        pairs = [
            ((c * ratio + m) * n_col + c, (c * ratio + m + t) % n_row * n_col + c)
            for c in range(n_col)
        ]
        out.append(lax.ppermute(value, BOTH, pairs))
    return out


def spread_choice(row, col, m, ratio):
    n_row, n_col = lax.axis_size("row"), lax.axis_size("col")
    if n_row == 4 and n_col == 4:
        apart = row ^ col
        return jnp.where(apart == 3, 2, jnp.where(apart == 0, 0, 1))
    return (row - (col * ratio + m) + n_row) % n_row


def to_owners(pieces, ratio):
    n_row, n_col = lax.axis_size("row"), lax.axis_size("col")
    row = lax.axis_index("row")
    if ratio > 1:
        stacked = jnp.stack(pieces)
        pieces = [
            lax.dynamic_index_in_dim(stacked, (row + t) % n_row, 0, keepdims=False)
            for t in range(n_row)
        ]
    parts = []
    for t, piece in enumerate(pieces):
        pairs = []
        for r in range(n_row):
            m, k = divmod((r + t) % n_row, n_col)
            pairs += [(r * n_col + c, (c * ratio + m) * n_col + k) for c in range(n_col)]
        parts.append(lax.ppermute(piece, BOTH, pairs))
    return parts


def one(value):
    return value[None].astype(jnp.int32)


def body(
    alignment,
    coverage,
    layer_norm_gain,
    layer_norm_bias,
    left_weight,
    right_weight,
    out_weight,
    out_bias,
    cotangent,
):
    n_row, n_col = lax.axis_size("row"), lax.axis_size("col")
    ratio = n_row // n_col
    row_index = lax.axis_index("row")
    col_index = lax.axis_index("col")
    me_row, me_col = one(row_index), one(col_index)
    seqs, rows, chans = alignment.shape
    narrow = left_weight.shape[1]
    pair = out_weight.shape[1]
    piece_rows = (seqs // n_col + 7) // 8 * 8
    cov_t = coverage.T
    wl_t, wr_t = left_weight.T, right_weight.T

    cov_far = [spread_small(cov_t, m, ratio) for m in range(ratio)]
    normed, xhat, stat, right = project(cov_t, alignment, layer_norm_gain, layer_norm_bias, wr_t)
    right, cov_far = lax.optimization_barrier((right, cov_far))

    right_pieces, firsts = [], []
    for m in range(ratio):
        own = one(row_index == col_index * ratio + m)
        turn_by = one(row_index) if ratio == 1 else jnp.zeros_like(me_row)
        scaled, grad_outer, w2, left_t, dcol, *pieces = right_side(
            own,
            turn_by,
            cov_t,
            cov_far[m],
            cotangent,
            out_weight,
            wl_t,
            normed,
            m,
            n_col,
            piece_rows,
        )
        firsts.append((scaled, grad_outer, w2, left_t, dcol))
        right_pieces.extend(pieces)
    right_parts = to_owners(right_pieces, ratio)

    left_pieces, updates, weight_pieces = None, [], None
    for m in range(ratio):
        scaled, grad_outer, w2, left_t, dcol = firsts[m]
        sel = one(spread_choice(row_index, col_index, m, ratio))
        right_cols, *pieces = left_side(
            sel, me_col, grad_outer, spread(right, m, ratio), n_col, piece_rows
        )
        update, *gw = forward(
            me_row, cov_t, left_t, right_cols, scaled, w2, dcol, out_bias, n_row
        )
        updates.append(update)
        if m == 0:
            left_pieces, weight_pieces = pieces, gw
        else:
            left_pieces = [(a.astype(F32) + b).astype(BF) for a, b in zip(left_pieces, pieces)]
            weight_pieces = [
                (a.astype(F32) + b).astype(a.dtype) for a, b in zip(weight_pieces, gw)
            ]
    pair_update = updates[0] if ratio == 1 else jnp.concatenate(updates, axis=1)

    gw_parts = shifts(weight_pieces[0], weight_pieces[1:], "row")
    lefts = shifts(left_pieces[0], left_pieces[1:], "col")
    lefts, pair_update = lax.optimization_barrier((lefts, pair_update))
    q = tokens(me_col, cov_t, stat, lefts, right_parts, normed)
    qs = gather(q, "col")

    if weight_pieces[0].shape[0] % (8 * n_col) == 0:
        pieces = cut(me_col, gw_parts, n_col)
        part = sum(shifts(pieces[0], pieces[1:], "col"))
        parts = [part] + [shift(part, "col", t) for t in range(1, n_col)]
    else:
        parts = [lax.psum(cut(me_col, gw_parts, 1)[0], "col")]
    ends = (xhat, wl_t, wr_t, layer_norm_gain)
    if n_col == 4:
        gradient = finish(me_col, [qs[0], qs[1]], *ends, 0, 2)
        gradient, parts = lax.optimization_barrier((gradient, parts))
    last = join_send(me_col, parts, qs, 2 * narrow)
    lasts = [last] + [shift(last, "row", t) for t in range(1, n_row)]
    if n_col == 4:
        gradient = finish(me_col, qs, *ends, 2, 2, gradient)
    else:
        gradient = finish(me_col, qs, *ends, 0, seqs // piece_rows)
    lasts, gradient = lax.optimization_barrier((lasts, gradient))
    grad_out, grad_left, grad_right = join_out(me_row, lasts, 2 * narrow, narrow)
    return pair_update, gradient, grad_left.T, grad_right.T, grad_out


def solution(mesh):
    return jax.shard_map(
        body,
        mesh=mesh,
        in_specs=(
            P("grp", "row", None),
            P("grp", "row"),
            P(),
            P(),
            P(),
            P(),
            P(),
            P(),
            P(("grp", "row"), "col", None),
        ),
        out_specs=(
            P(("grp", "row"), "col", None),
            P("grp", "row", None),
            P("grp", None),
            P("grp", None),
            P("grp", None),
        ),
        check_vma=False,
    )
```
